128 devices in a mesh: leaf: 16 (over x, y), sub: 8 (over z, core).
Axes of the slice: x: 4, y: 4, z: 4, core: 2. Of those that a mesh axis runs over, the one named last changes fastest.
Arguments:
- points: float32 [32, 524288], P(None, ('leaf', 'sub')), may hold values from -6 to 6
- right_side: float32 [16, 524288], P(None, ('leaf', 'sub')), may hold values from -6 to 6
- interp: float32 [1024, 512, 128], P(('leaf', 'sub')), may hold values from -0.5 to 0.5
- leaf_skel: int32 [1024, 128], P(('leaf', 'sub')), may hold values from 0 to 511, as said below
- up_one: float32 [512, 256, 128], P(('leaf', 'sub')), may hold values from -0.375 to 0.375
- skel_one: int32 [512, 128], P(('leaf', 'sub')), may hold values from 0 to 255, as said below
- up_two: float32 [256, 256, 128], P(('leaf', 'sub')), may hold values from -0.375 to 0.375
- skel_two: int32 [256, 128], P(('leaf', 'sub')), may hold values from 0 to 255, as said below
- up_three: float32 [128, 256, 128], P(('leaf', 'sub')), may hold values from -0.375 to 0.375
- skel_three: int32 [128, 128], P(('leaf', 'sub')), may hold values from 0 to 255, as said below
- up_top: float32 [96, 256, 128], replicated, may hold values from -0.375 to 0.375
- skel_top: int32 [96, 128], replicated, may hold values from 0 to 255, as said below
- near_list: int32 [1024, 12], P(('leaf', 'sub')), may hold values from 0 to 1023, as said below
- far_three: int32 [128, 2], P(('leaf', 'sub')), may hold values from 0 to 127, as said below
- far_top: int32 [96, 4], replicated, may hold values from 0 to 95, as said below
Outputs:
- solution: float32 [16, 524288], P(None, ('leaf', 'sub'))
- residual: float32 [16, 524288], P(None, ('leaf', 'sub'))
The draws below stay inside these ranges and needn't reach their ends.
Inputs may be any that keep to these rules, and one draw needn't show every extreme that they name: `leaf_skel`: each row holds 128 different positions among the leaf's 512 points. `skel_one`: each row holds 128 different positions among the two children's 2 * 128 skeleton points. `skel_two`: each row holds 128 different positions among the two children's 2 * 128 skeleton points. `skel_three`: each row holds 128 different positions among the two children's 2 * 128 skeleton points. `skel_top`: each row holds 128 different positions among the two children's 2 * 128 skeleton points. `near_list`: row a lists different leaves b with b != a and |b - a| <= 8 in its first slots and a in the remaining ones; in every draw some leaf fills all 12 slots. `far_three`: row n lists n - 1 or n + 1 or both in its first slots and n in the remaining ones; in every draw some node fills both slots. `far_top`: row t lists different nodes of t's own level other than t in its first slots and t in the remaining ones; on each level some node fills all 4 slots in every draw.
All inputs are finite; a program needn't handle non-finite values.
Results may differ from the reference program's by a relative error of at most 0.0003.
Values sent between devices are 32-bit elements; how exact they have to be, the bound alone decides.
No kernel may reach another device: no remote copies, remote signals or barrier semaphores. Data moves between devices by JAX's collectives and lax.ppermute only.
A program may use at most 128 MiB of HBM per device.

```python
import jax
import jax.numpy as jnp
from jax import lax

LEAF = 512
DIMS = 32
RIGHT_HAND_COUNT = 16
RANK = 128
LEAF_DEV = 8
NEAR_MAX = 12
TOP_MAX = 4
ITERS = 2
LEAVES = 1024
POINT_TOTAL = 524288
NODES_ONE = 512
NODES_TWO = 256
NODES_THREE = 128
NODES_FOUR = 64
NODES_FIVE = 32
NODES_TOP = 96


def distinct_pick(seed_key, row_count, span, chosen_count):
    scores = jax.random.randint(seed_key, (row_count, span), 0, 1 << 20) * span + jnp.arange(span, dtype=jnp.int32)[None, :]
    ordering = jnp.argsort(scores, axis=1)
    return ordering[:, :chosen_count].astype(jnp.int32)


def draw_leaf_skel(key, part):
    key = jax.random.fold_in(key, 11)
    return distinct_pick(key, LEAVES, LEAF, RANK)


def draw_skel_one(key, part):
    key = jax.random.fold_in(key, 12)
    return distinct_pick(key, NODES_ONE, 2 * RANK, RANK)


def draw_skel_two(key, part):
    key = jax.random.fold_in(key, 13)
    return distinct_pick(key, NODES_TWO, 2 * RANK, RANK)


def draw_skel_three(key, part):
    key = jax.random.fold_in(key, 14)
    return distinct_pick(key, NODES_THREE, 2 * RANK, RANK)


def draw_skel_top(key, part):
    key = jax.random.fold_in(key, 15)
    return distinct_pick(key, NODES_TOP, 2 * RANK, RANK)


def draw_near_list(key, part):
    key = jax.random.fold_in(key, 21)
    key_order, key_number, key_heavy, key_forced = jax.random.split(key, 4)
    offsets = jnp.concatenate([jnp.arange(-LEAF_DEV, 0), jnp.arange(1, LEAF_DEV + 1)]).astype(jnp.int32)
    span = 2 * LEAF_DEV
    leaf_ids = jnp.arange(LEAVES, dtype=jnp.int32)
    targets = leaf_ids[:, None] + offsets[None, :]
    inner_points = (targets >= 0) & (targets < LEAVES)
    scores = jax.random.randint(key_order, (LEAVES, span), 0, 1 << 20) * span + jnp.arange(span, dtype=jnp.int32)[None, :]
    scores = jnp.where(inner_points, scores, (1 << 30) + jnp.arange(span, dtype=jnp.int32)[None, :])
    ordering = jnp.argsort(scores, axis=1)
    chosen = jnp.take_along_axis(targets, ordering, axis=1)[:, :NEAR_MAX]
    heavy = jax.random.randint(key_heavy, (LEAVES // LEAF_DEV,), 0, 4) == 0
    ceiling = jnp.repeat(jnp.where(heavy, NEAR_MAX, 3), LEAF_DEV)
    number = jax.random.randint(key_number, (LEAVES,), 0, 1 << 20) % ceiling + 1
    forced = jax.random.randint(key_forced, (), LEAF_DEV, LEAVES - LEAF_DEV)
    number = jnp.where(leaf_ids == forced, NEAR_MAX, number)
    number = jnp.minimum(number, jnp.sum(inner_points.astype(jnp.int32), 1))
    slot_ids = jnp.arange(NEAR_MAX, dtype=jnp.int32)[None, :]
    return jnp.where(slot_ids < number[:, None], chosen, leaf_ids[:, None]).astype(jnp.int32)


def draw_far_three(key, part):
    key = jax.random.fold_in(key, 22)
    key_pick, key_forced = jax.random.split(key)
    node_ids = jnp.arange(NODES_THREE, dtype=jnp.int32)
    left_ok = node_ids > 0
    right_ok = node_ids < NODES_THREE - 1
    coin_side = jax.random.randint(key_pick, (NODES_THREE,), 0, 3)
    forced = jax.random.randint(key_forced, (), 1, NODES_THREE - 1)
    coin_side = jnp.where(node_ids == forced, 2, coin_side)
    use_left = ((coin_side == 0) | (coin_side == 2)) & left_ok
    use_right = ((coin_side == 1) | (coin_side == 2)) & right_ok
    use_left = use_left | ~use_right & left_ok
    use_right = use_right | ~use_left & right_ok
    leading = jnp.where(use_left, node_ids - 1, jnp.where(use_right, node_ids + 1, node_ids))
    trailing = jnp.where(use_left & use_right, node_ids + 1, node_ids)
    return jnp.stack([leading, trailing], 1).astype(jnp.int32)


def level_lists(seed_key, node_total, offset_base):
    key_order, key_number, key_forced = jax.random.split(seed_key, 3)
    node_ids = jnp.arange(node_total, dtype=jnp.int32)
    scores = jax.random.randint(key_order, (node_total, node_total), 0, 1 << 20) * node_total + node_ids[None, :]
    scores = jnp.where(node_ids[:, None] == node_ids[None, :], 1 << 30, scores)
    ordering = jnp.argsort(scores, axis=1)[:, :TOP_MAX].astype(jnp.int32)
    number = jax.random.randint(key_number, (node_total,), 1, TOP_MAX + 1)
    forced = jax.random.randint(key_forced, (), 0, node_total)
    number = jnp.where(node_ids == forced, TOP_MAX, number)
    slot_ids = jnp.arange(TOP_MAX, dtype=jnp.int32)[None, :]
    return jnp.where(slot_ids < number[:, None], ordering, node_ids[:, None]) + offset_base


def draw_far_top(key, part):
    key = jax.random.fold_in(key, 23)
    key_four, key_five = jax.random.split(key)
    return jnp.concatenate([level_lists(key_four, NODES_FOUR, 0), level_lists(key_five, NODES_FIVE, NODES_FOUR)], 0).astype(jnp.int32)


def steps_of(rng, extent, shards, least, high):
    gain, own = 1.0, jax.random.fold_in(rng, 6)
    for position, blocks in shards:
        draws = jnp.exp(jax.random.uniform(jax.random.fold_in(own, position), (blocks,), jnp.float32, least / len(shards), high / len(shards)))
        gain = gain * jnp.repeat(draws, extent[position] // blocks).reshape([-1 if axis == position else 1 for axis in range(len(extent))])
    return gain


def scatter_about(own_key, extent, scale, reach, cuts=(), held_as=jnp.bfloat16):
    result = jax.random.normal(own_key, extent, jnp.float32) * scale
    if len(cuts) > 0:
        result = steps_of(own_key, extent, cuts, -0.22, 0.18) * result
    return jnp.clip(result, min=-reach, max=reach).astype(held_as)


def setup_inputs(seed: int = 0) -> dict:
    arg_keys = jax.random.split(jax.random.key(seed), 16)
    points = scatter_about(arg_keys[0], (DIMS, POINT_TOTAL), 1.0, 6.0, ((1, 128),), jnp.float32)
    right_side = scatter_about(arg_keys[1], (RIGHT_HAND_COUNT, POINT_TOTAL), 1.0, 6.0, ((1, 128),), jnp.float32)
    interp = scatter_about(arg_keys[2], (LEAVES, LEAF, RANK), RANK ** -0.5, 0.5, ((0, 128),), jnp.float32)
    leaf_skel = draw_leaf_skel(jax.random.fold_in(arg_keys[15], 71), 0)
    up_one = scatter_about(arg_keys[4], (NODES_ONE, 2 * RANK, RANK), (2 * RANK) ** -0.5, 0.375, ((0, 128),), jnp.float32)
    skel_one = draw_skel_one(jax.random.fold_in(arg_keys[15], 71), 0)
    up_two = scatter_about(arg_keys[6], (NODES_TWO, 2 * RANK, RANK), (2 * RANK) ** -0.5, 0.375, ((0, 128),), jnp.float32)
    skel_two = draw_skel_two(jax.random.fold_in(arg_keys[15], 71), 0)
    up_three = scatter_about(arg_keys[8], (NODES_THREE, 2 * RANK, RANK), (2 * RANK) ** -0.5, 0.375, ((0, 128),), jnp.float32)
    skel_three = draw_skel_three(jax.random.fold_in(arg_keys[15], 71), 0)
    up_top = scatter_about(arg_keys[10], (NODES_TOP, 2 * RANK, RANK), (2 * RANK) ** -0.5, 0.375, (), jnp.float32)
    skel_top = draw_skel_top(jax.random.fold_in(arg_keys[15], 71), 0)
    near_list = draw_near_list(jax.random.fold_in(arg_keys[15], 71), 0)
    far_three = draw_far_three(jax.random.fold_in(arg_keys[15], 71), 0)
    far_top = draw_far_top(jax.random.fold_in(arg_keys[15], 71), 0)
    return dict(points=points, right_side=right_side, interp=interp, leaf_skel=leaf_skel, up_one=up_one, skel_one=skel_one, up_two=up_two, skel_two=skel_two, up_three=up_three, skel_three=skel_three, up_top=up_top, skel_top=skel_top, near_list=near_list, far_three=far_three, far_top=far_top)


RIDGE_TERM = 12.0
KERNEL_SPREAD = 24.0
exact_answer = lax.Precision.HIGHEST


def kernel_pair(left_pts, right_pts):
    left_sq = jnp.sum(left_pts * left_pts, 0)
    right_sq = jnp.sum(right_pts * right_pts, 0)
    cross_dot = jnp.einsum('dm,dn->mn', left_pts, right_pts, precision=exact_answer)
    return jnp.exp(-(left_sq[:, None] + right_sq[None, :] - 2.0 * cross_dot) / KERNEL_SPREAD)


def lift(child_rows, weights):
    node_count = weights.shape[0]
    stacked = child_rows.reshape(node_count, 2 * RANK, RIGHT_HAND_COUNT)
    return jnp.einsum('nks,nkr->nsr', weights, stacked, precision=exact_answer)


def select(child_rows, chosen):
    node_count = chosen.shape[0]
    paired = child_rows.reshape(node_count, 2, DIMS, RANK).transpose(0, 2, 1, 3).reshape(node_count, DIMS, 2 * RANK)
    return jnp.take_along_axis(paired, chosen[:, None, :], axis=2)


def lower(weights, parent):
    node_count = weights.shape[0]
    spread = jnp.einsum('nks,nsr->nkr', weights, parent, precision=exact_answer)
    return spread.reshape(2 * node_count, RANK, RIGHT_HAND_COUNT)


def interact(own_skel, pool_skel, pool_charges, partners, self_ids):
    own_sq = jnp.sum(own_skel * own_skel, 1)
    running = jnp.zeros((own_skel.shape[0], RANK, RIGHT_HAND_COUNT), jnp.float32)
    for slot_index in range(partners.shape[1]):
        other_ids = partners[:, slot_index]
        weight = (other_ids != self_ids).astype(jnp.float32)
        other_skel = jnp.take(pool_skel, other_ids, axis=0)
        other_sq = jnp.sum(other_skel * other_skel, 1)
        cross_dot = jnp.einsum('kdi,kdj->kij', own_skel, other_skel, precision=exact_answer)
        block = jnp.exp(-(own_sq[:, :, None] + other_sq[:, None, :] - 2.0 * cross_dot) / KERNEL_SPREAD) * weight[:, None, None]
        running = running + jnp.einsum('kij,kjr->kir', block, jnp.take(pool_charges, other_ids, axis=0), precision=exact_answer)
    return running


def reference(points, right_side, interp, leaf_skel, up_one, skel_one, up_two, skel_two, up_three, skel_three, up_top, skel_top, near_list, far_three, far_top):
    cloud = points.reshape(DIMS, LEAVES, LEAF)
    leaves_first = cloud.transpose(1, 0, 2)
    skel_base = jnp.take_along_axis(leaves_first, leaf_skel[:, None, :], axis=2)
    skel_mid = select(select(select(skel_base, skel_one), skel_two), skel_three)
    skel_four = select(skel_mid, skel_top[:NODES_FOUR])
    skel_five = select(skel_four, skel_top[NODES_FOUR:])
    skel_upper = jnp.concatenate([skel_four, skel_five], 0)
    mid_ids = jnp.arange(NODES_THREE, dtype=jnp.int32)
    top_ids = jnp.arange(NODES_TOP, dtype=jnp.int32)

    def near_field(vectors):
        target_values = vectors.reshape(RIGHT_HAND_COUNT, LEAVES, LEAF)

        def one_leaf(leaf_index):
            own_pts = cloud[:, leaf_index]
            running = jnp.einsum('rj,ji->ri', target_values[:, leaf_index], kernel_pair(own_pts, own_pts), precision=exact_answer)
            for slot_index in range(NEAR_MAX):
                other_id = near_list[leaf_index, slot_index]
                mark_slot = (other_id != leaf_index).astype(jnp.float32)
                block = kernel_pair(cloud[:, other_id], own_pts) * mark_slot
                running = running + jnp.einsum('rj,ji->ri', target_values[:, other_id], block, precision=exact_answer)
            return running

        rows_out = lax.map(one_leaf, jnp.arange(LEAVES, dtype=jnp.int32))
        return rows_out.transpose(1, 0, 2).reshape(RIGHT_HAND_COUNT, POINT_TOTAL)

    def far_field(vectors):
        target_values = vectors.reshape(RIGHT_HAND_COUNT, LEAVES, LEAF)
        source_charges = jnp.einsum('gxm,fgx->gmf', interp, target_values, precision=exact_answer)
        mid_charges = lift(lift(lift(source_charges, up_one), up_two), up_three)
        charge_four = lift(mid_charges, up_top[:NODES_FOUR])
        charge_five = lift(charge_four, up_top[NODES_FOUR:])
        middle_field = interact(skel_mid, skel_mid, mid_charges, far_three, mid_ids)
        field_top = interact(skel_upper, skel_upper, jnp.concatenate([charge_four, charge_five], 0), far_top, top_ids)
        down_four = field_top[:NODES_FOUR] + lower(up_top[NODES_FOUR:], field_top[NODES_FOUR:])
        down_mid = middle_field + lower(up_top[:NODES_FOUR], down_four)
        downward_leaf = lower(up_one, lower(up_two, lower(up_three, down_mid)))
        return jnp.einsum('uwz,uza->auw', interp, downward_leaf, precision=exact_answer).reshape(RIGHT_HAND_COUNT, POINT_TOTAL)

    def apply(vectors):
        return RIDGE_TERM * vectors + near_field(vectors) + far_field(vectors)

    solution = jnp.zeros_like(right_side)
    residual = right_side
    direction = right_side
    norm_now = jnp.sum(residual * residual, 1)
    for turn_index in range(ITERS):
        mapped = apply(direction)
        step_size = norm_now / jnp.sum(direction * mapped, 1)
        solution = solution + step_size[:, None] * direction
        residual = residual - step_size[:, None] * mapped
        norm_next = jnp.sum(residual * residual, 1)
        direction = residual + (norm_next / norm_now)[:, None] * direction
        norm_now = norm_next
    return solution, residual
```

```python
import functools
import math

import jax
import jax.numpy as jnp
from jax import lax
from jax.experimental import pallas as pl
from jax.experimental.pallas import tpu as pltpu
from jax.sharding import PartitionSpec as P

LEAF = 512
DIMS = 32
RHS = 16
RANK = 128
LEAVES_HERE = 8
SLOTS = 12
WIDTH = LEAVES_HERE * LEAF
DEVICES = 128
NODES_FOUR = 64
TOP_SLOTS = 4

RIDGE_TERM = 12.0
COORD_SCALE = math.sqrt(2.0 * math.log2(math.e) / 24.0)

AXES = ("leaf", "sub")
BF = jnp.bfloat16
F = jnp.float32
NN = (((1,), (0,)), ((), ()))
NT = (((1,), (1,)), ((), ()))
VMEM = pl.BlockSpec(memory_space=pltpu.VMEM)
SMEM = pl.BlockSpec(memory_space=pltpu.SMEM)
ANY = pl.BlockSpec(memory_space=pl.ANY)


def shape(dims, dtype=F):
    return jax.ShapeDtypeStruct(dims, dtype)


def mm(a, b, dims=NN):
    return lax.dot_general(a, b, dims, preferred_element_type=F)


def split_two(x):
    high = x.astype(BF)
    return high, (x - high.astype(F)).astype(BF)


def split_three(x):
    high = x.astype(BF)
    rest = x - high.astype(F)
    mid = rest.astype(BF)
    return high, mid, (rest - mid.astype(F)).astype(BF)


def dot_split(a, w, dims=NN):
    ah, am = split_two(a)
    wh, wm = split_two(w)
    both = mm(jnp.concatenate([ah, am], 0), wh, dims)
    return both[:RHS] + both[RHS:] + mm(ah, wm, dims)


def operands(y):
    n = y.shape[1]
    h, m, l = split_three(y)
    half = 0.5 * jnp.sum(y * y, 0, keepdims=True)
    parts = [p.astype(F) for p in split_three(half)]
    one = [jnp.ones((1, n), F)] * 3
    pad = [jnp.zeros((10, n), F)]
    tail_left = jnp.concatenate(parts + one + pad, 0).astype(BF)
    tail_right = jnp.concatenate([-p for p in one + parts] + pad, 0).astype(BF)
    zero = jnp.zeros((48, n), BF)
    left = jnp.concatenate([h, h, m, h, l, m, tail_left, zero], 0)
    right = jnp.concatenate([h, m, h, l, h, m, tail_right, zero], 0)
    return left, right


def pick(parts, chosen):
    n = parts.shape[1]
    rows = lax.broadcasted_iota(jnp.int32, (n, RANK), 0)
    hot = jnp.where(rows == chosen, 1.0, 0.0).astype(BF)
    return mm(parts, hot).astype(BF)


def joined(parts):
    return parts[0:32].astype(F) + parts[32:64].astype(F) + parts[64:96].astype(F)


def parts_of(y):
    return jnp.concatenate(split_three(y), 0)


def prep_kernel(x_ref, leaf_ref, one_ref, two_ref, three_ref, right_ref, left_ref, skel_ref):
    level = []
    for a in range(LEAVES_HERE):
        y = x_ref[:, a * LEAF : (a + 1) * LEAF] * COORD_SCALE
        left, right = operands(y)
        left_ref[a] = left
        right_ref[a] = right.T
        level.append(pick(parts_of(y), leaf_ref[a : a + 1, :]))
    for ref in (one_ref, two_ref, three_ref):
        level = [
            pick(jnp.concatenate([level[2 * n], level[2 * n + 1]], 1), ref[n : n + 1, :])
            for n in range(len(level) // 2)
        ]
    skel_ref[...] = joined(level[0])


def prep(points, leaf_skel, skel_one, skel_two, skel_three):
    return pl.pallas_call(
        prep_kernel,
        out_shape=[
            shape((LEAVES_HERE, LEAF, 256), BF),
            shape((LEAVES_HERE, 256, LEAF), BF),
            shape((DIMS, RANK)),
        ],
        in_specs=[VMEM] * 5,
        out_specs=[VMEM] * 3,
        compiler_params=pltpu.CompilerParams(vmem_limit_bytes=40 << 20),
        cost_estimate=pl.CostEstimate(flops=2 * 10**9, bytes_accessed=5 << 20, transcendentals=0),
        name="prep_own",
    )(points, leaf_skel, skel_one, skel_two, skel_three)


def prep_near_kernel(low_ref, high_ref, right_ref):
    for side, ref in enumerate((low_ref, high_ref)):
        for a in range(LEAVES_HERE):
            y = ref[:, a * LEAF : (a + 1) * LEAF] * COORD_SCALE
            right_ref[side * LEAVES_HERE + a] = operands(y)[1].T


def prep_near(low, high):
    return pl.pallas_call(
        prep_near_kernel,
        out_shape=shape((2 * LEAVES_HERE, LEAF, 256), BF),
        in_specs=[VMEM] * 2,
        out_specs=VMEM,
        compiler_params=pltpu.CompilerParams(vmem_limit_bytes=40 << 20),
        cost_estimate=pl.CostEstimate(flops=2 * 10**9, bytes_accessed=5 << 20, transcendentals=0),
        name="prep_beside",
    )(low, high)


def near_kernel(cross, *refs):
    if cross:
        (dev_ref, list_ref, right_ref, left_ref, low_ref, high_ref, start_ref, out_ref) = refs[:8]
        sources = (low_ref, high_ref)
    else:
        (dev_ref, list_ref, right_ref, left_ref, own_ref, out_ref) = refs[:6]
        sources = (own_ref,)
    total, values, ea, eb, targets, origins = refs[-6:]
    count = len(sources) * LEAVES_HERE
    first = dev_ref[0] * LEAVES_HERE

    for side, ref in enumerate(sources):
        for a in range(LEAVES_HERE):
            values[side * LEAVES_HERE + a] = jnp.concatenate(
                split_three(ref[:, a * LEAF : (a + 1) * LEAF]), 0
            )
    values[count] = jnp.zeros((3 * RHS, LEAF), BF)
    total[...] = jnp.zeros_like(total)

    def collect(a, n):
        if not cross:
            targets[n] = a
            origins[n] = a
            n = n + 1
        for slot in range(SLOTS):
            place = list_ref[a, slot] - first
            inside = (place >= 0) & (place < LEAVES_HERE)
            if cross:
                use = jnp.logical_not(inside)
                origin = jnp.where(place < 0, place + LEAVES_HERE, place)
            else:
                use = inside & (place != a)
                origin = place
            targets[n] = a
            origins[n] = origin
            n = n + use.astype(jnp.int32)
        return n

    filled = lax.fori_loop(0, LEAVES_HERE, collect, jnp.int32(0))
    for extra in range(3):
        targets[filled + extra] = 0
        origins[filled + extra] = count

    def exponent(t):
        return mm(right_ref[jnp.minimum(origins[t], count - 1)], left_ref[targets[t]])

    def add(t, e):
        a = targets[t]
        v = values[origins[t]]
        block = jnp.exp2(e)
        high = block.astype(BF)
        low = (block - high.astype(F)).astype(BF)
        total[a, 0:32] += mm(v[:32], high)
        total[a, 0:16] += mm(v[:16], low)

    ea[...] = exponent(0)

    def pair(p, carry):
        t = 2 * p
        eb[...] = exponent(t + 1)
        add(t, ea[...])
        ea[...] = exponent(t + 2)
        add(t + 1, eb[...])
        return carry

    lax.fori_loop(0, (filled + 1) // 2, pair, 0)
    for a in range(LEAVES_HERE):
        cols = slice(a * LEAF, (a + 1) * LEAF)
        result = total[a, 0:16] + total[a, 16:32]
        if cross:
            result = start_ref[:, cols] + result
        out_ref[:, cols] = result


def near(cross, device, near_list, right, left, *fields):
    count = LEAVES_HERE * (2 if cross else 1)
    return pl.pallas_call(
        functools.partial(near_kernel, cross),
        out_shape=shape((RHS, WIDTH)),
        in_specs=[SMEM, SMEM] + [VMEM] * (2 + len(fields)),
        out_specs=VMEM,
        scratch_shapes=[
            pltpu.VMEM((LEAVES_HERE, 32, LEAF), F),
            pltpu.VMEM((count + 1, 3 * RHS, LEAF), BF),
            pltpu.VMEM((LEAF, LEAF), F),
            pltpu.VMEM((LEAF, LEAF), F),
            pltpu.SMEM((LEAVES_HERE * (SLOTS + 1) + 8,), jnp.int32),
            pltpu.SMEM((LEAVES_HERE * (SLOTS + 1) + 8,), jnp.int32),
        ],
        compiler_params=pltpu.CompilerParams(vmem_limit_bytes=40 << 20),
        cost_estimate=pl.CostEstimate(
            flops=20 * 10**9, bytes_accessed=8 << 20, transcendentals=30 * LEAF * LEAF
        ),
        name="near_beside" if cross else "near_own",
    )(device, near_list, right, left, *fields)


def row_of_sums(products):
    folded = []
    for value in products:
        piece = value[:, 0:RANK]
        for t in range(1, WIDTH // RANK):
            piece = piece + value[:, t * RANK : (t + 1) * RANK]
        folded.append(piece)
    rest = RANK - RHS * len(folded)
    stacked = jnp.concatenate(folded + [jnp.zeros((rest, RANK), F)], 0)
    return jnp.sum(stacked.T, 0, keepdims=True)


def up_kernel(sums, *refs):
    if sums:
        v_ref, base_ref, interp_ref, one_ref, two_ref, three_ref, out_ref = refs
    else:
        v_ref, interp_ref, one_ref, two_ref, three_ref, out_ref = refs
    level = [
        dot_split(v_ref[:, a * LEAF : (a + 1) * LEAF], interp_ref[a]) for a in range(LEAVES_HERE)
    ]
    for ref in (one_ref, two_ref, three_ref):
        level = [
            dot_split(jnp.concatenate([level[2 * n], level[2 * n + 1]], 1), ref[n])
            for n in range(len(level) // 2)
        ]
    message = level[0]
    if sums:
        base = base_ref[...]
        row = row_of_sums([base * base, base * v_ref[...]])
        message = jnp.concatenate([message, row, jnp.zeros((7, RANK), F)], 0)
    out_ref[...] = jnp.broadcast_to(message[None], out_ref.shape)


def up(sums, fields, interp, up_one, up_two, up_three):
    rows = RHS + (8 if sums else 0)
    return pl.pallas_call(
        functools.partial(up_kernel, sums),
        out_shape=shape((DEVICES, rows, RANK)),
        in_specs=[VMEM] * (len(fields) + 4),
        out_specs=VMEM,
        compiler_params=pltpu.CompilerParams(vmem_limit_bytes=40 << 20),
        cost_estimate=pl.CostEstimate(flops=10**9, bytes_accessed=5 << 20, transcendentals=0),
        name="up_sums" if sums else "up",
    )(*fields, interp, up_one, up_two, up_three)


def skel_kernel(dev_ref, three_ref, top_ref, skel_ref, index_ref, out_ref):
    dev = dev_ref[0]

    def base(n):
        return parts_of(skel_ref[n])

    def four(n):
        both = jnp.concatenate([base(2 * n), base(2 * n + 1)], 1)
        return pick(both, index_ref[pl.ds(n, 1), :])

    def five(n):
        both = jnp.concatenate([four(2 * n), four(2 * n + 1)], 1)
        return pick(both, index_ref[pl.ds(NODES_FOUR + n, 1), :])

    def block(slot, own_left, other, weight):
        right = operands(joined(other))[1]
        out_ref[slot] = jnp.exp2(mm(right.T, own_left)) * weight

    node_four = dev // 2
    node_five = dev // 4
    left = operands(skel_ref[dev])[0]
    for s in range(2):
        other = three_ref[0, s]
        block(s, left, base(other), jnp.where(other != dev, 1.0, 0.0))
    left = operands(joined(four(node_four)))[0]
    for s in range(TOP_SLOTS):
        other = top_ref[node_four, s]
        block(2 + s, left, four(other), jnp.where(other != node_four, 1.0, 0.0))
    left = operands(joined(five(node_five)))[0]
    for s in range(TOP_SLOTS):
        other = top_ref[NODES_FOUR + node_five, s] - NODES_FOUR
        block(6 + s, left, five(other), jnp.where(other != node_five, 1.0, 0.0))


def skeleton_blocks(device, far_three, far_top, skels, skel_top):
    return pl.pallas_call(
        skel_kernel,
        out_shape=shape((2 + 2 * TOP_SLOTS, RANK, RANK)),
        in_specs=[SMEM, SMEM, SMEM, VMEM, VMEM],
        out_specs=VMEM,
        compiler_params=pltpu.CompilerParams(vmem_limit_bytes=40 << 20),
        cost_estimate=pl.CostEstimate(flops=10**9, bytes_accessed=4 << 20, transcendentals=163840),
        name="skeleton_blocks",
    )(device, far_three, far_top, skels, skel_top)


def down_kernel(last, *refs):
    (dev_ref, three_ref, top_ref, message_ref, block_ref, up_top_ref) = refs[:6]
    (interp_ref, one_ref, two_ref, up_three_ref, field_ref, near_ref) = refs[6:12]
    if last:
        base_ref, out_ref, row_ref, weights, arrived = refs[12:]
    else:
        out_ref, weights, arrived = refs[12:]
    dev = dev_ref[0]
    node_four = dev // 2
    node_five = dev // 4
    fours = [top_ref[node_four, s] for s in range(TOP_SLOTS)]
    fives = [top_ref[NODES_FOUR + node_five, s] - NODES_FOUR for s in range(TOP_SLOTS)]
    wanted = []
    for n in fives:
        wanted += [2 * n, 2 * n + 1, NODES_FOUR + n]
    wanted += fours
    wanted += [NODES_FOUR + node_five, node_four]
    copies = [
        pltpu.make_async_copy(up_top_ref.at[n], weights.at[i], arrived.at[i])
        for i, n in enumerate(wanted)
    ]
    for copy in copies:
        copy.start()

    def charge(n):
        return message_ref[n, 0:RHS, :]

    def lift(n, weight):
        return dot_split(jnp.concatenate([charge(2 * n), charge(2 * n + 1)], 1), weight)

    field_three = jnp.zeros((RHS, RANK), F)
    for s in range(2):
        field_three = field_three + dot_split(charge(three_ref[0, s]), block_ref[s])
    for copy in copies:
        copy.wait()
    field_five = jnp.zeros((RHS, RANK), F)
    for s, n in enumerate(fives):
        low = lift(2 * n, weights[3 * s])
        high = lift(2 * n + 1, weights[3 * s + 1])
        q = dot_split(jnp.concatenate([low, high], 1), weights[3 * s + 2])
        field_five = field_five + dot_split(q, block_ref[6 + s])
    field_four = jnp.zeros((RHS, RANK), F)
    for s, n in enumerate(fours):
        q = lift(n, weights[12 + s])
        field_four = field_four + dot_split(q, block_ref[2 + s])

    def half(i, side):
        return weights[i, pl.ds(pl.multiple_of(side * RANK, RANK), RANK), :]

    field_four = field_four + dot_split(field_five, half(16, node_four % 2), NT)
    level = [field_three + dot_split(field_four, half(17, dev % 2), NT)]
    for ref in (up_three_ref, two_ref, one_ref):
        spread = [dot_split(h, ref[n], NT) for n, h in enumerate(level)]
        level = [s[:, side * RANK : (side + 1) * RANK] for s in spread for side in range(2)]
    for a in range(LEAVES_HERE):
        cols = slice(a * LEAF, (a + 1) * LEAF)
        far = dot_split(level[a], interp_ref[a], NT)
        out_ref[:, cols] = RIDGE_TERM * field_ref[:, cols] + near_ref[:, cols] + far
    if last:
        step = first_step(jnp.sum(message_ref[:, RHS : RHS + 8, :], 0))
        image = field_ref[...]
        residual = base_ref[...] - step * image
        moved = image - step * out_ref[...]
        row = row_of_sums(
            [residual * residual, residual * moved, base_ref[...] * moved, residual * image]
        )
        row_ref[...] = jnp.broadcast_to(row, row_ref.shape)


def columns(row_block):
    return row_block.T[:, 0:1]


def first_step(row_block):
    sums = columns(row_block)
    return sums[0:RHS] / sums[RHS : 2 * RHS]


def down(last, device, far_three, far_top, message, blocks, up_top, weights, field, near_part, base):
    out = [shape((RHS, WIDTH))]
    extra = []
    if last:
        out.append(shape((DEVICES, RANK)))
        extra = [base]
    return pl.pallas_call(
        functools.partial(down_kernel, last),
        out_shape=out,
        in_specs=[SMEM] * 3 + [VMEM] * 2 + [ANY] + [VMEM] * (6 + len(extra)),
        out_specs=[VMEM] * len(out),
        scratch_shapes=[pltpu.VMEM((18, 2 * RANK, RANK), F), pltpu.SemaphoreType.DMA((18,))],
        compiler_params=pltpu.CompilerParams(vmem_limit_bytes=40 << 20),
        cost_estimate=pl.CostEstimate(flops=10**9, bytes_accessed=9 << 20, transcendentals=0),
        name="down_sums" if last else "down",
    )(device, far_three, far_top, message, blocks, up_top, *weights, field, near_part, *extra)


def finish_kernel(rows_ref, message_ref, base_ref, image_ref, second_ref, solution_ref, residual_ref):
    before = columns(jnp.sum(message_ref[:, RHS : RHS + 8, :], 0))
    rows = jnp.sum(rows_ref[...], 0, keepdims=True)
    after = columns(jnp.broadcast_to(rows, (8, RANK)))
    norm, curvature = before[0:RHS], before[RHS : 2 * RHS]
    step = norm / curvature
    norm_next, rm, bm, ri = [after[q * RHS : (q + 1) * RHS] for q in range(4)]
    turn = norm_next / norm
    second_curvature = rm + turn * (bm + ri + turn * curvature)
    second_step = norm_next / second_curvature
    base = base_ref[...]
    image = image_ref[...]
    residual = base - step * image
    direction = residual + turn * base
    moved = image - step * second_ref[...] + turn * image
    solution_ref[...] = step * base + second_step * direction
    residual_ref[...] = residual - second_step * moved


def finish(rows, message, base, image, second):
    return pl.pallas_call(
        finish_kernel,
        out_shape=[shape((RHS, WIDTH))] * 2,
        in_specs=[VMEM] * 5,
        out_specs=[VMEM] * 2,
        compiler_params=pltpu.CompilerParams(vmem_limit_bytes=40 << 20),
        cost_estimate=pl.CostEstimate(flops=10**6, bytes_accessed=4 << 20, transcendentals=0),
        name="finish",
    )(rows, message, base, image, second)


def beside(value):
    forward = [(i, i + 1) for i in range(DEVICES - 1)]
    backward = [(target, source) for source, target in forward]
    return lax.ppermute(value, AXES, forward), lax.ppermute(value, AXES, backward)


def everyone(copies):
    return lax.all_to_all(copies, AXES, 0, 0, tiled=True)


def local(
    points,
    right_side,
    interp,
    leaf_skel,
    up_one,
    skel_one,
    up_two,
    skel_two,
    up_three,
    skel_three,
    up_top,
    skel_top,
    near_list,
    far_three,
    far_top,
):
    device = lax.axis_index(AXES).astype(jnp.int32).reshape(1)
    weights = (interp, up_one, up_two, up_three)
    points_low, points_high = beside(points)
    base_low, base_high = beside(right_side)
    right, left, skel = prep(points, leaf_skel, skel_one, skel_two, skel_three)
    skels = everyone(jnp.broadcast_to(skel[None], (DEVICES, DIMS, RANK)))
    message = everyone(up(False, (right_side,), *weights))
    part = near(False, device, near_list, right, left, right_side)
    right_beside = prep_near(points_low, points_high)
    part = near(True, device, near_list, right_beside, left, base_low, base_high, part)
    blocks = skeleton_blocks(device, far_three, far_top, skels, skel_top)
    (image,) = down(
        False, device, far_three, far_top, message, blocks, up_top, weights, right_side, part, None
    )
    image_low, image_high = beside(image)
    message = everyone(up(True, (image, right_side), *weights))
    part = near(False, device, near_list, right, left, image)
    part = near(True, device, near_list, right_beside, left, image_low, image_high, part)
    second, rows = down(
        True, device, far_three, far_top, message, blocks, up_top, weights, image, part, right_side
    )
    rows = everyone(rows)
    return tuple(finish(rows, message, right_side, image, second))


def solution(mesh):
    both = ("leaf", "sub")
    placed = (
        P(None, both),
        P(None, both),
        P(both, None, None),
        P(both, None),
        P(both, None, None),
        P(both, None),
        P(both, None, None),
        P(both, None),
        P(both, None, None),
        P(both, None),
        P(),
        P(),
        P(both, None),
        P(both, None),
        P(),
    )
    return jax.shard_map(
        local,
        mesh=mesh,
        in_specs=placed,
        out_specs=(P(None, both), P(None, both)),
        check_vma=False,
    )
```

```python
import functools
import math

import jax
import jax.numpy as jnp
from jax import lax
from jax.experimental import pallas as pl
from jax.experimental.pallas import tpu as pltpu
from jax.sharding import PartitionSpec as P

LEAF = 512
DIMS = 32
RHS = 16
RANK = 128
LEAVES_HERE = 8
SLOTS = 12
WIDTH = LEAVES_HERE * LEAF
DEVICES = 128
NODES_FOUR = 64
TOP_SLOTS = 4
AT_THREE, AT_FOUR, AT_FIVE, AT_NEAR = 1, 3, 7, 16

RIDGE_TERM = 12.0
COORD_SCALE = math.sqrt(2.0 * math.log2(math.e) / 24.0)

AXES = ("leaf", "sub")
BF = jnp.bfloat16
F = jnp.float32
NN = (((1,), (0,)), ((), ()))
NT = (((1,), (1,)), ((), ()))
SMEM = pl.BlockSpec(memory_space=pltpu.SMEM)
ANY = pl.BlockSpec(memory_space=pl.ANY)


def shape(dims, dtype=F):
    return jax.ShapeDtypeStruct(dims, dtype)


def mm(a, b, dims=NN):
    return lax.dot_general(a, b, dims, preferred_element_type=F)


def split_two(x):
    high = x.astype(BF)
    return high, (x - high.astype(F)).astype(BF)


def split_three(x):
    high = x.astype(BF)
    rest = x - high.astype(F)
    mid = rest.astype(BF)
    return high, mid, (rest - mid.astype(F)).astype(BF)


def dot_split(a, w, dims=NN):
    ah, am = split_two(a)
    wh, wm = split_two(w)
    both = mm(jnp.concatenate([ah, am], 0), wh, dims)
    return both[:RHS] + both[RHS:] + mm(ah, wm, dims)


def operands(y):
    n = y.shape[1]
    h, m, l = split_three(y)
    half = 0.5 * jnp.sum(y * y, 0, keepdims=True)
    parts = [p.astype(F) for p in split_three(half)]
    one = [jnp.ones((1, n), F)] * 3
    pad = [jnp.zeros((10, n), F)]
    tail_left = jnp.concatenate(parts + one + pad, 0).astype(BF)
    tail_right = jnp.concatenate([-p for p in one + parts] + pad, 0).astype(BF)
    zero = jnp.zeros((48, n), BF)
    left = jnp.concatenate([h, h, m, h, l, m, tail_left, zero], 0)
    right = jnp.concatenate([h, m, h, l, h, m, tail_right, zero], 0)
    return left, right


def pick(parts, chosen):
    n = parts.shape[1]
    rows = lax.broadcasted_iota(jnp.int32, (n, RANK), 0)
    hot = jnp.where(rows == chosen, 1.0, 0.0).astype(BF)
    return mm(parts, hot).astype(BF)


def joined(parts):
    return parts[0:32].astype(F) + parts[32:64].astype(F) + parts[64:96].astype(F)


def parts_of(y):
    return jnp.concatenate(split_three(y), 0)


class Copies:
    def __init__(self, semaphores):
        self.semaphores = semaphores
        self.used = 0

    def start(self, source, target):
        copy = pltpu.make_async_copy(source, target, self.semaphores.at[self.used])
        self.used += 1
        copy.start()
        return copy


def wait_all(copies):
    for copy in copies:
        copy.wait()


def call(kernel, name, out, ids, inputs, scratch, flops, transcendentals=0):
    operands_given = ([ids] if ids is not None else []) + list(inputs)
    return pl.pallas_call(
        kernel,
        out_shape=out,
        in_specs=([SMEM] if ids is not None else []) + [ANY] * len(inputs),
        out_specs=[ANY] * len(out),
        scratch_shapes=scratch + [pltpu.SemaphoreType.DMA((48,))],
        compiler_params=pltpu.CompilerParams(vmem_limit_bytes=56 << 20),
        cost_estimate=pl.CostEstimate(
            flops=flops, bytes_accessed=6 << 20, transcendentals=transcendentals
        ),
        name=name,
    )(*operands_given)


def scratch_for(arrays):
    return [pltpu.VMEM(a.shape, a.dtype) for a in arrays]


def cols(a):
    return slice(a * LEAF, (a + 1) * LEAF)


def row_of_sums(products):
    folded = []
    for value in products:
        piece = value[:, 0:RANK]
        for t in range(1, WIDTH // RANK):
            piece = piece + value[:, t * RANK : (t + 1) * RANK]
        folded.append(piece)
    rest = RANK - RHS * len(folded)
    stacked = jnp.concatenate(folded + [jnp.zeros((rest, RANK), F)], 0)
    return jnp.sum(stacked.T, 0, keepdims=True)


def climb(field, interp, transfers):
    level = [dot_split(field[:, cols(a)], interp[a]) for a in range(LEAVES_HERE)]
    for ref in transfers:
        level = [
            dot_split(jnp.concatenate([level[2 * n], level[2 * n + 1]], 1), ref[n])
            for n in range(len(level) // 2)
        ]
    return level[0]


def first_kernel(*refs):
    inputs, (message_out, halo_out) = refs[:10], refs[10:12]
    held, (message, semaphores) = refs[12:22], refs[22:]
    copies = Copies(semaphores)
    arrive = [copies.start(source, target) for source, target in zip(inputs, held)]
    points, field, interp, one, two, three, leaf_pick, one_pick, two_pick, three_pick = held
    wait_all(arrive[0:2])
    leave = [
        copies.start(points, halo_out.at[0:DIMS, :]),
        copies.start(field, halo_out.at[DIMS : DIMS + RHS, :]),
    ]
    wait_all(arrive[6:])
    level = [
        pick(parts_of(points[:, cols(a)] * COORD_SCALE), leaf_pick[a : a + 1, :])
        for a in range(LEAVES_HERE)
    ]
    for ref in (one_pick, two_pick, three_pick):
        level = [
            pick(jnp.concatenate([level[2 * n], level[2 * n + 1]], 1), ref[n : n + 1, :])
            for n in range(len(level) // 2)
        ]
    wait_all(arrive[2:6])
    charges = climb(field, interp, (one, two, three))
    block = jnp.concatenate([charges, joined(level[0])], 0)
    message[...] = jnp.broadcast_to(block[None], message.shape)
    leave += send_copies(copies, message, message_out)
    wait_all(leave)


def send_copies(copies, message, message_out):
    count = message.shape[0]
    return [
        copies.start(message, message_out.at[t * count : (t + 1) * count])
        for t in range(DEVICES // count)
    ]


def first(points, right_side, weights, picks):
    inputs = [points, right_side, *weights, *picks]
    return call(
        first_kernel,
        "first_up",
        [shape((DEVICES, RHS + DIMS, RANK)), shape((DIMS + RHS, WIDTH))],
        None,
        inputs,
        scratch_for(inputs) + [pltpu.VMEM((16, RHS + DIMS, RANK), F)],
        10**9,
    )


def near_kernel(fresh, *refs):
    if fresh:
        ids_ref, points_in, field_in, low_in, high_in, part_out, right_out, left_out = refs[:8]
        points, field, low, high = refs[8:12]
    else:
        ids_ref, right_in, left_in, field_in, low_in, high_in, part_out = refs[:7]
        field, low, high = refs[7:10]
    right, left, total, values, ea, eb, part, targets, origins, semaphores = refs[-10:]
    copies = Copies(semaphores)
    arrive_field = copies.start(field_in, field)
    if fresh:
        arrive_own = [copies.start(points_in, points)]
    else:
        arrive_own = [
            copies.start(left_in, left),
            copies.start(right_in.at[0:LEAVES_HERE], right.at[0:LEAVES_HERE]),
        ]
    arrive_beside = [copies.start(low_in, low), copies.start(high_in, high)]
    if not fresh:
        arrive_beside.append(
            copies.start(
                right_in.at[LEAVES_HERE : 3 * LEAVES_HERE], right.at[LEAVES_HERE : 3 * LEAVES_HERE]
            )
        )
    first = ids_ref[0] * LEAVES_HERE
    empty = 3 * LEAVES_HERE
    beside_at = 128

    def collect(a, counts):
        n, m = counts
        targets[n] = a
        origins[n] = a
        n = n + 1
        for slot in range(SLOTS):
            place = ids_ref[AT_NEAR + a * SLOTS + slot] - first
            inside = (place >= 0) & (place < LEAVES_HERE)
            targets[n] = a
            origins[n] = place
            n = n + (inside & (place != a)).astype(jnp.int32)
            targets[m] = a
            origins[m] = jnp.where(place < 0, place + 2 * LEAVES_HERE, place + LEAVES_HERE)
            m = m + jnp.logical_not(inside).astype(jnp.int32)
        return n, m

    own_end, beside_end = lax.fori_loop(
        0, LEAVES_HERE, collect, (jnp.int32(0), jnp.int32(beside_at))
    )
    for end in (own_end, beside_end):
        for extra in range(3):
            targets[end + extra] = 0
            origins[end + extra] = empty

    def take_values(source, at):
        for a in range(LEAVES_HERE):
            values[at + a] = jnp.concatenate(split_three(source[source.shape[0] - RHS :, cols(a)]), 0)

    def exponent(t):
        origin = origins[t]
        return mm(right[jnp.where(origin == empty, 0, origin)], left[targets[t]])

    def add(t, e):
        a = targets[t]
        v = values[origins[t]]
        block = jnp.exp2(e)
        upper = block.astype(BF)
        lower = (block - upper.astype(F)).astype(BF)
        total[a, 0:32] += mm(v[:32], upper)
        total[a, 0:16] += mm(v[:16], lower)

    def run(start, end):
        ea[...] = exponent(start)

        def pair(p, carry):
            t = start + 2 * p
            eb[...] = exponent(t + 1)
            add(t, ea[...])
            ea[...] = exponent(t + 2)
            add(t + 1, eb[...])
            return carry

        lax.fori_loop(0, (end - start + 1) // 2, pair, 0)

    total[...] = jnp.zeros_like(total)
    values[empty] = jnp.zeros((3 * RHS, LEAF), BF)
    wait_all([arrive_field])
    take_values(field, 0)
    wait_all(arrive_own)
    leave = []
    if fresh:
        for a in range(LEAVES_HERE):
            left_part, right_part = operands(points[:, cols(a)] * COORD_SCALE)
            left[a] = left_part
            right[a] = right_part.T
        leave.append(copies.start(left, left_out))
        leave.append(copies.start(right.at[0:LEAVES_HERE], right_out.at[0:LEAVES_HERE]))
    run(0, own_end)
    wait_all(arrive_beside)
    take_values(low, LEAVES_HERE)
    take_values(high, 2 * LEAVES_HERE)
    if fresh:
        for side, source in enumerate((low, high)):
            for a in range(LEAVES_HERE):
                y = source[0:DIMS, cols(a)] * COORD_SCALE
                right[(side + 1) * LEAVES_HERE + a] = operands(y)[1].T
        beside = slice(LEAVES_HERE, 3 * LEAVES_HERE)
        leave.append(copies.start(right.at[beside], right_out.at[beside]))
    run(beside_at, beside_end)
    for a in range(LEAVES_HERE):
        part[:, cols(a)] = total[a, 0:16] + total[a, 16:32]
    leave.append(copies.start(part, part_out))
    wait_all(leave)


def near(fresh, ids, *inputs):
    right = shape((3 * LEAVES_HERE, LEAF, 256), BF)
    left = shape((LEAVES_HERE, 256, LEAF), BF)
    held = inputs if fresh else inputs[2:]
    return call(
        functools.partial(near_kernel, fresh),
        "near_first" if fresh else "near_second",
        [shape((RHS, WIDTH))] + ([right, left] if fresh else []),
        ids,
        inputs,
        scratch_for(held)
        + scratch_for([right, left])
        + [
            pltpu.VMEM((LEAVES_HERE, 32, LEAF), F),
            pltpu.VMEM((3 * LEAVES_HERE + 1, 3 * RHS, LEAF), BF),
            pltpu.VMEM((LEAF, LEAF), F),
            pltpu.VMEM((LEAF, LEAF), F),
            pltpu.VMEM((RHS, WIDTH), F),
            pltpu.SMEM((256,), jnp.int32),
            pltpu.SMEM((256,), jnp.int32),
        ],
        40 * 10**9,
        50 * LEAF * LEAF,
    )


def first_step(row_block):
    sums = columns(row_block)
    return sums[0:RHS] / sums[RHS : 2 * RHS]


def columns(row_block):
    return row_block.T[:, 0:1]


def down_kernel(fresh, *refs):
    ids_ref, message_in, blocks_in, up_top_in = refs[:4]
    if fresh:
        sources, (image_out, message_out, blocks_out) = refs[4:10], refs[10:13]
        refs = refs[13:]
    else:
        sources, (image_out, rows_out, sums_out) = refs[4:11], refs[11:14]
        refs = refs[14:]
    held, refs = refs[: len(sources)], refs[len(sources) :]
    weights, nodes, image, semaphores = refs[0], refs[1], refs[2], refs[-1]
    copies = Copies(semaphores)
    dev = ids_ref[0]
    node_four = dev // 2
    node_five = dev // 4
    threes = [ids_ref[AT_THREE + s] for s in range(2)]
    fours = [ids_ref[AT_FOUR + s] for s in range(TOP_SLOTS)]
    fives = [ids_ref[AT_FIVE + s] for s in range(TOP_SLOTS)]

    early = []
    if fresh:
        picks, made = refs[3], refs[4]
        early.append(copies.start(blocks_in, picks))
        blocks = made
    else:
        blocks, all_sums, row = refs[3], refs[4], refs[5]
        early.append(copies.start(blocks_in, blocks))
        arrive_sums = copies.start(message_in.at[:, RHS : RHS + 8, :], all_sums)
    for s, n in enumerate(fives):
        early.append(copies.start(message_in.at[pl.ds(4 * n, 4)], nodes.at[4 * s : 4 * s + 4]))
    for s, n in enumerate(fours):
        early.append(
            copies.start(message_in.at[pl.ds(2 * n, 2)], nodes.at[16 + 2 * s : 18 + 2 * s])
        )
    for s, n in enumerate(threes):
        early.append(copies.start(message_in.at[pl.ds(n, 1)], nodes.at[24 + s : 25 + s]))
    if fresh:
        early.append(copies.start(message_in.at[pl.ds(4 * node_five, 4)], nodes.at[26:30]))
    arrive = []
    for s, n in enumerate(fives):
        arrive.append(copies.start(up_top_in.at[pl.ds(2 * n, 2)], weights.at[3 * s : 3 * s + 2]))
        arrive.append(
            copies.start(
                up_top_in.at[pl.ds(NODES_FOUR + n, 1)], weights.at[3 * s + 2 : 3 * s + 3]
            )
        )
    for s, n in enumerate(fours + [node_four, NODES_FOUR + node_five]):
        arrive.append(copies.start(up_top_in.at[pl.ds(n, 1)], weights.at[12 + s : 13 + s]))
    arrive += [copies.start(source, target) for source, target in zip(sources, held)]
    interp, one, two, three, field, near_part = held[:6]
    wait_all(early)

    def pair_of(at, get):
        return jnp.concatenate([get(at), get(at + 1)], 1)

    if fresh:

        def base(at):
            return parts_of(nodes[at, RHS : RHS + DIMS, :])

        def four(at, n):
            return pick(pair_of(at, base), picks[pl.ds(n, 1), :])

        def five(at, n):
            both = jnp.concatenate([four(at, 2 * n), four(at + 2, 2 * n + 1)], 1)
            return pick(both, picks[pl.ds(NODES_FOUR + n, 1), :])

        def block(slot, own_left, other, differs):
            right = operands(joined(other))[1]
            made[slot] = jnp.exp2(mm(right.T, own_left)) * jnp.where(differs, 1.0, 0.0)

        own = operands(nodes[26 + dev % 4, RHS : RHS + DIMS, :])[0]
        for s, n in enumerate(threes):
            block(s, own, base(24 + s), n != dev)
        own = operands(joined(four(26 + 2 * (node_four % 2), node_four)))[0]
        for s, n in enumerate(fours):
            block(2 + s, own, four(16 + 2 * s, n), n != node_four)
        own = operands(joined(five(26, node_five)))[0]
        for s, n in enumerate(fives):
            block(6 + s, own, five(4 * s, n), n != node_five)
        leave = [copies.start(made, blocks_out)]
    else:
        leave = []

    def charge(at):
        return nodes[at, 0:RHS, :]

    field_three = jnp.zeros((RHS, RANK), F)
    for s in range(2):
        field_three = field_three + dot_split(charge(24 + s), blocks[s])
    wait_all(arrive)
    field_five = jnp.zeros((RHS, RANK), F)
    for s in range(TOP_SLOTS):
        lower = dot_split(pair_of(4 * s, charge), weights[3 * s])
        upper = dot_split(pair_of(4 * s + 2, charge), weights[3 * s + 1])
        q = dot_split(jnp.concatenate([lower, upper], 1), weights[3 * s + 2])
        field_five = field_five + dot_split(q, blocks[6 + s])
    field_four = jnp.zeros((RHS, RANK), F)
    for s in range(TOP_SLOTS):
        q = dot_split(pair_of(16 + 2 * s, charge), weights[12 + s])
        field_four = field_four + dot_split(q, blocks[2 + s])

    def half(at, side):
        return weights[at, pl.ds(pl.multiple_of(side * RANK, RANK), RANK), :]

    field_four = field_four + dot_split(field_five, half(17, node_four % 2), NT)
    level = [field_three + dot_split(field_four, half(16, dev % 2), NT)]
    for ref in (three, two, one):
        spread = [dot_split(h, ref[n], NT) for n, h in enumerate(level)]
        level = [s[:, side * RANK : (side + 1) * RANK] for s in spread for side in range(2)]
    for a in range(LEAVES_HERE):
        far = dot_split(level[a], interp[a], NT)
        image[:, cols(a)] = RIDGE_TERM * field[:, cols(a)] + near_part[:, cols(a)] + far
    leave.append(copies.start(image, image_out))
    if fresh:
        message = refs[5]
        charges = climb(image, interp, (one, two, three))
        sums = row_of_sums([field[...] * field[...], field[...] * image[...]])
        block = jnp.concatenate([charges, sums, jnp.zeros((7, RANK), F)], 0)
        message[...] = jnp.broadcast_to(block[None], message.shape)
        leave += send_copies(copies, message, message_out)
    else:
        wait_all([arrive_sums])
        base_field = held[6]
        all_sums[0] = jnp.sum(all_sums[...], 0)
        step = first_step(all_sums[0])
        residual = base_field[...] - step * field[...]
        moved = field[...] - step * image[...]
        sums = row_of_sums(
            [residual * residual, residual * moved, base_field[...] * moved, residual * field[...]]
        )
        row[...] = jnp.broadcast_to(sums, row.shape)
        leave.append(copies.start(row, rows_out))
        leave.append(copies.start(all_sums.at[0], sums_out))
    wait_all(leave)


def down(fresh, ids, message, blocks, up_top, *sources):
    made = shape((2 + 2 * TOP_SLOTS, RANK, RANK))
    rows = message.shape[1]
    scratch = scratch_for(sources) + [
        pltpu.VMEM((18, 2 * RANK, RANK), F),
        pltpu.VMEM((30, rows, RANK), F),
        pltpu.VMEM((RHS, WIDTH), F),
    ]
    if fresh:
        out = [shape((RHS, WIDTH)), shape((DEVICES, RHS + 8, RANK)), made]
        scratch += [
            pltpu.VMEM(blocks.shape, jnp.int32),
            pltpu.VMEM(made.shape, F),
            pltpu.VMEM((16, RHS + 8, RANK), F),
        ]
    else:
        out = [shape((RHS, WIDTH)), shape((DEVICES, RANK)), shape((8, RANK))]
        scratch += [
            pltpu.VMEM(made.shape, F),
            pltpu.VMEM((DEVICES, 8, RANK), F),
            pltpu.VMEM((DEVICES, RANK), F),
        ]
    return call(
        functools.partial(down_kernel, fresh),
        "down_first" if fresh else "down_second",
        out,
        ids,
        [message, blocks, up_top, *sources],
        scratch,
        10**9,
    )


def finish_kernel(*refs):
    inputs, (solution_out, residual_out) = refs[:5], refs[5:7]
    held, (solution_held, residual_held, semaphores) = refs[7:12], refs[12:]
    copies = Copies(semaphores)
    wait_all([copies.start(source, target) for source, target in zip(inputs, held)])
    rows_ref, sums_ref, base_ref, image_ref, second_ref = held
    before = columns(sums_ref[...])
    rows = jnp.sum(rows_ref[...], 0, keepdims=True)
    after = columns(jnp.broadcast_to(rows, (8, RANK)))
    norm, curvature = before[0:RHS], before[RHS : 2 * RHS]
    step = norm / curvature
    norm_next, rm, bm, ri = [after[q * RHS : (q + 1) * RHS] for q in range(4)]
    turn = norm_next / norm
    second_curvature = rm + turn * (bm + ri + turn * curvature)
    second_step = norm_next / second_curvature
    base = base_ref[...]
    image = image_ref[...]
    residual = base - step * image
    direction = residual + turn * base
    moved = image - step * second_ref[...] + turn * image
    solution_held[...] = step * base + second_step * direction
    leave = [copies.start(solution_held, solution_out)]
    residual_held[...] = residual - second_step * moved
    leave.append(copies.start(residual_held, residual_out))
    wait_all(leave)


def finish(*inputs):
    out = [shape((RHS, WIDTH))] * 2
    return call(finish_kernel, "finish", out, None, inputs, scratch_for(inputs) + scratch_for(out), 10**6)


def beside(value):
    forward = [(i, i + 1) for i in range(DEVICES - 1)]
    backward = [(target, source) for source, target in forward]
    return lax.ppermute(value, AXES, forward), lax.ppermute(value, AXES, backward)


def everyone(copies):
    return lax.all_to_all(copies, AXES, 0, 0, tiled=True)


def local(
    points,
    right_side,
    interp,
    leaf_skel,
    up_one,
    skel_one,
    up_two,
    skel_two,
    up_three,
    skel_three,
    up_top,
    skel_top,
    near_list,
    far_three,
    far_top,
):
    device = lax.axis_index(AXES).astype(jnp.int32)
    fours = lax.dynamic_index_in_dim(far_top, device // 2, 0, False)
    fives = lax.dynamic_index_in_dim(far_top, NODES_FOUR + device // 4, 0, False) - NODES_FOUR
    ids = jnp.concatenate(
        [device[None], far_three[0], fours, fives, jnp.zeros((5,), jnp.int32), near_list.reshape(-1)]
    )
    weights = (interp, up_one, up_two, up_three)
    message, halo = first(
        points, right_side, weights, (leaf_skel, skel_one, skel_two, skel_three)
    )
    low, high = beside(halo)
    message = everyone(message)
    part, right, left = near(True, ids, points, right_side, low, high)
    image, own_message, blocks = down(
        True, ids, message, skel_top, up_top, *weights, right_side, part
    )
    low, high = beside(image)
    message = everyone(own_message)
    (part,) = near(False, ids, right, left, image, low, high)
    second, rows, sums = down(
        False, ids, message, blocks, up_top, *weights, image, part, right_side
    )
    return tuple(finish(everyone(rows), sums, right_side, image, second))


def solution(mesh):
    both = ("leaf", "sub")
    placed = (
        P(None, both),
        P(None, both),
        P(both, None, None),
        P(both, None),
        P(both, None, None),
        P(both, None),
        P(both, None, None),
        P(both, None),
        P(both, None, None),
        P(both, None),
        P(),
        P(),
        P(both, None),
        P(both, None),
        P(),
    )
    return jax.shard_map(
        local,
        mesh=mesh,
        in_specs=placed,
        out_specs=(P(None, both), P(None, both)),
        check_vma=False,
    )
```

```python
import functools
import math

import jax
import jax.numpy as jnp
from jax import lax
from jax.experimental import pallas as pl
from jax.experimental.pallas import tpu as pltpu
from jax.sharding import PartitionSpec as P

LEAF = 512
DIMS = 32
RHS = 16
RANK = 128
LEAVES_HERE = 8
SLOTS = 12
WIDTH = LEAVES_HERE * LEAF
DEVICES = 128
NODES_FOUR = 64
TOP_SLOTS = 4
AT_THREE, AT_FOUR, AT_FIVE, AT_NEAR = 1, 3, 7, 16

RIDGE_TERM = 12.0
COORD_SCALE = math.sqrt(2.0 * math.log2(math.e) / 24.0)

AXES = ("leaf", "sub")
BF = jnp.bfloat16
F = jnp.float32
NN = (((1,), (0,)), ((), ()))
NT = (((1,), (1,)), ((), ()))
SMEM = pl.BlockSpec(memory_space=pltpu.SMEM)
ANY = pl.BlockSpec(memory_space=pl.ANY)


def shape(dims, dtype=F):
    return jax.ShapeDtypeStruct(dims, dtype)


def mm(a, b, dims=NN):
    return lax.dot_general(a, b, dims, preferred_element_type=F)


def split_two(x):
    high = x.astype(BF)
    return high, (x - high.astype(F)).astype(BF)


def split_three(x):
    high = x.astype(BF)
    rest = x - high.astype(F)
    mid = rest.astype(BF)
    return high, mid, (rest - mid.astype(F)).astype(BF)


def dot_split(a, w, dims=NN):
    ah, am = split_two(a)
    wh, wm = split_two(w)
    both = mm(jnp.concatenate([ah, am], 0), wh, dims)
    return both[:RHS] + both[RHS:] + mm(ah, wm, dims)


def operands(y):
    n = y.shape[1]
    h, m, l = split_three(y)
    half = 0.5 * jnp.sum(y * y, 0, keepdims=True)
    parts = [p.astype(F) for p in split_three(half)]
    one = [jnp.ones((1, n), F)] * 3
    pad = [jnp.zeros((10, n), F)]
    tail_left = jnp.concatenate(parts + one + pad, 0).astype(BF)
    tail_right = jnp.concatenate([-p for p in one + parts] + pad, 0).astype(BF)
    zero = jnp.zeros((48, n), BF)
    left = jnp.concatenate([h, h, m, h, l, m, tail_left, zero], 0)
    right = jnp.concatenate([h, m, h, l, h, m, tail_right, zero], 0)
    return left, right


def pick(parts, chosen):
    n = parts.shape[1]
    rows = lax.broadcasted_iota(jnp.int32, (n, RANK), 0)
    hot = jnp.where(rows == chosen, 1.0, 0.0).astype(BF)
    return mm(parts, hot).astype(BF)


def joined(parts):
    return parts[0:32].astype(F) + parts[32:64].astype(F) + parts[64:96].astype(F)


def parts_of(y):
    return jnp.concatenate(split_three(y), 0)


class Copies:
    def __init__(self, semaphores):
        self.semaphores = semaphores
        self.used = 0

    def start(self, source, target):
        copy = pltpu.make_async_copy(source, target, self.semaphores.at[self.used])
        self.used += 1
        copy.start()
        return copy


def wait_all(copies):
    for copy in copies:
        copy.wait()


def call(kernel, name, out, ids, inputs, scratch, flops, transcendentals=0):
    operands_given = ([ids] if ids is not None else []) + list(inputs)
    return pl.pallas_call(
        kernel,
        out_shape=out,
        in_specs=([SMEM] if ids is not None else []) + [ANY] * len(inputs),
        out_specs=[ANY] * len(out),
        scratch_shapes=scratch + [pltpu.SemaphoreType.DMA((48,))],
        compiler_params=pltpu.CompilerParams(vmem_limit_bytes=63 << 20),
        cost_estimate=pl.CostEstimate(
            flops=flops, bytes_accessed=6 << 20, transcendentals=transcendentals
        ),
        name=name,
    )(*operands_given)


def scratch_for(arrays):
    return [pltpu.VMEM(a.shape, a.dtype) for a in arrays]


def cols(a):
    return slice(a * LEAF, (a + 1) * LEAF)


def row_of_sums(products):
    folded = []
    for value in products:
        piece = value[:, 0:RANK]
        for t in range(1, WIDTH // RANK):
            piece = piece + value[:, t * RANK : (t + 1) * RANK]
        folded.append(piece)
    rest = RANK - RHS * len(folded)
    stacked = jnp.concatenate(folded + [jnp.zeros((rest, RANK), F)], 0)
    return jnp.sum(stacked.T, 0, keepdims=True)


def climb(field, interp, transfers):
    level = [dot_split(field[:, cols(a)], interp[a]) for a in range(LEAVES_HERE)]
    for ref in transfers:
        level = [
            dot_split(jnp.concatenate([level[2 * n], level[2 * n + 1]], 1), ref[n])
            for n in range(len(level) // 2)
        ]
    return level[0]


def first_kernel(*refs):
    inputs, (message_out, halo_out) = refs[:10], refs[10:12]
    held, (message, semaphores) = refs[12:22], refs[22:]
    copies = Copies(semaphores)
    arrive = [copies.start(source, target) for source, target in zip(inputs, held)]
    points, field, interp, one, two, three, leaf_pick, one_pick, two_pick, three_pick = held
    wait_all(arrive[0:2])
    leave = [
        copies.start(points, halo_out.at[0:DIMS, :]),
        copies.start(field, halo_out.at[DIMS : DIMS + RHS, :]),
    ]
    wait_all(arrive[6:])
    level = [
        pick(parts_of(points[:, cols(a)] * COORD_SCALE), leaf_pick[a : a + 1, :])
        for a in range(LEAVES_HERE)
    ]
    for ref in (one_pick, two_pick, three_pick):
        level = [
            pick(jnp.concatenate([level[2 * n], level[2 * n + 1]], 1), ref[n : n + 1, :])
            for n in range(len(level) // 2)
        ]
    wait_all(arrive[2:6])
    charges = climb(field, interp, (one, two, three))
    block = jnp.concatenate([charges, joined(level[0])], 0)
    message[...] = jnp.broadcast_to(block[None], message.shape)
    leave += send_copies(copies, message, message_out)
    wait_all(leave)


def send_copies(copies, message, message_out):
    count = message.shape[0]
    return [
        copies.start(message, message_out.at[t * count : (t + 1) * count])
        for t in range(DEVICES // count)
    ]


def first(points, right_side, weights, picks):
    inputs = [points, right_side, *weights, *picks]
    return call(
        first_kernel,
        "first_up",
        [shape((DEVICES, RHS + DIMS, RANK)), shape((DIMS + RHS, WIDTH))],
        None,
        inputs,
        scratch_for(inputs) + [pltpu.VMEM((16, RHS + DIMS, RANK), F)],
        10**9,
    )


def near_kernel(fresh, *refs):
    if fresh:
        ids_ref, points_in, field_in, partner_in, other_in, part_out, right_out, left_out = refs[:8]
        points, field, partner, other = refs[8:12]
    else:
        ids_ref, right_in, left_in, field_in, partner_in, other_in, part_out = refs[:7]
        field, partner, other = refs[7:10]
    right, left, total, values, ea, eb, part, targets, origins, semaphores = refs[-10:]
    copies = Copies(semaphores)
    arrive_field = copies.start(field_in, field)
    if fresh:
        arrive_own = [copies.start(points_in, points)]
    else:
        arrive_own = [
            copies.start(left_in, left),
            copies.start(right_in.at[0:LEAVES_HERE], right.at[0:LEAVES_HERE]),
        ]
    arrive_beside = [copies.start(partner_in, partner), copies.start(other_in, other)]
    if not fresh:
        arrive_beside.append(
            copies.start(
                right_in.at[LEAVES_HERE : 3 * LEAVES_HERE], right.at[LEAVES_HERE : 3 * LEAVES_HERE]
            )
        )
    first = ids_ref[0] * LEAVES_HERE
    empty = 3 * LEAVES_HERE
    beside_at = 128
    odd = ids_ref[0] % 2 == 1
    shift_low = jnp.where(odd, 2 * LEAVES_HERE, 3 * LEAVES_HERE)
    shift_high = jnp.where(odd, LEAVES_HERE, 0)

    def collect(a, counts):
        n, m = counts
        targets[n] = a
        origins[n] = a
        n = n + 1
        for slot in range(SLOTS):
            place = ids_ref[AT_NEAR + a * SLOTS + slot] - first
            inside = (place >= 0) & (place < LEAVES_HERE)
            targets[n] = a
            origins[n] = place
            n = n + (inside & (place != a)).astype(jnp.int32)
            targets[m] = a
            origins[m] = place + jnp.where(place < 0, shift_low, shift_high)
            m = m + jnp.logical_not(inside).astype(jnp.int32)
        return n, m

    own_end, beside_end = lax.fori_loop(
        0, LEAVES_HERE, collect, (jnp.int32(0), jnp.int32(beside_at))
    )
    for end in (own_end, beside_end):
        for extra in range(4):
            targets[end + extra] = 0
            origins[end + extra] = empty

    def take_values(source, at):
        for a in range(LEAVES_HERE):
            values[at + a] = jnp.concatenate(split_three(source[source.shape[0] - RHS :, cols(a)]), 0)

    def exponent(t):
        origin = origins[t]
        return mm(right[jnp.where(origin == empty, 0, origin)], left[targets[t]])

    def add(t, e):
        a = targets[t]
        v = values[origins[t]]
        block = jnp.exp2(e)
        upper = block.astype(BF)
        lower = (block - upper.astype(F)).astype(BF)
        total[a, 0:32] += mm(v[:32], upper)
        total[a, 0:16] += mm(v[:16], lower)

    def run(start, end):
        ea[...] = exponent(start)

        def pair(t):
            eb[...] = exponent(t + 1)
            add(t, ea[...])
            ea[...] = exponent(t + 2)
            add(t + 1, eb[...])

        def four(p, carry):
            pair(start + 4 * p)
            pair(start + 4 * p + 2)
            return carry

        def two(p, carry):
            pair(middle + 2 * p)
            return carry

        fours = (end - start) // 4
        middle = start + 4 * fours
        lax.fori_loop(0, fours, four, 0)
        lax.fori_loop(0, (end - middle + 1) // 2, two, 0)

    total[...] = jnp.zeros_like(total)
    values[empty] = jnp.zeros((3 * RHS, LEAF), BF)
    wait_all([arrive_field])
    take_values(field, 0)
    wait_all(arrive_own)
    leave = []
    if fresh:
        for a in range(LEAVES_HERE):
            left_part, right_part = operands(points[:, cols(a)] * COORD_SCALE)
            left[a] = left_part
            right[a] = right_part.T
        leave.append(copies.start(left, left_out))
        leave.append(copies.start(right.at[0:LEAVES_HERE], right_out.at[0:LEAVES_HERE]))
    run(0, own_end)
    wait_all(arrive_beside)
    take_values(partner, LEAVES_HERE)
    take_values(other, 2 * LEAVES_HERE)
    if fresh:
        for side, source in enumerate((partner, other)):
            for a in range(LEAVES_HERE):
                y = source[0:DIMS, cols(a)] * COORD_SCALE
                right[(side + 1) * LEAVES_HERE + a] = operands(y)[1].T
        beside = slice(LEAVES_HERE, 3 * LEAVES_HERE)
        leave.append(copies.start(right.at[beside], right_out.at[beside]))
    run(beside_at, beside_end)
    for a in range(LEAVES_HERE):
        part[:, cols(a)] = total[a, 0:16] + total[a, 16:32]
    leave.append(copies.start(part, part_out))
    wait_all(leave)


def near(fresh, ids, *inputs):
    right = shape((3 * LEAVES_HERE, LEAF, 256), BF)
    left = shape((LEAVES_HERE, 256, LEAF), BF)
    held = inputs if fresh else inputs[2:]
    return call(
        functools.partial(near_kernel, fresh),
        "near_first" if fresh else "near_second",
        [shape((RHS, WIDTH))] + ([right, left] if fresh else []),
        ids,
        inputs,
        scratch_for(held)
        + scratch_for([right, left])
        + [
            pltpu.VMEM((LEAVES_HERE, 32, LEAF), F),
            pltpu.VMEM((3 * LEAVES_HERE + 1, 3 * RHS, LEAF), BF),
            pltpu.VMEM((LEAF, LEAF), F),
            pltpu.VMEM((LEAF, LEAF), F),
            pltpu.VMEM((RHS, WIDTH), F),
            pltpu.SMEM((256,), jnp.int32),
            pltpu.SMEM((256,), jnp.int32),
        ],
        40 * 10**9,
        50 * LEAF * LEAF,
    )


def first_step(row_block):
    sums = columns(row_block)
    return sums[0:RHS] / sums[RHS : 2 * RHS]


def columns(row_block):
    return row_block.T[:, 0:1]


def down_kernel(fresh, *refs):
    ids_ref, message_in, blocks_in, up_top_in = refs[:4]
    if fresh:
        sources, (image_out, message_out, blocks_out) = refs[4:10], refs[10:13]
        refs = refs[13:]
    else:
        sources, (image_out, rows_out, sums_out) = refs[4:11], refs[11:14]
        refs = refs[14:]
    held, refs = refs[: len(sources)], refs[len(sources) :]
    weights, nodes, image, semaphores = refs[0], refs[1], refs[2], refs[-1]
    copies = Copies(semaphores)
    dev = ids_ref[0]
    node_four = dev // 2
    node_five = dev // 4
    threes = [ids_ref[AT_THREE + s] for s in range(2)]
    fours = [ids_ref[AT_FOUR + s] for s in range(TOP_SLOTS)]
    fives = [ids_ref[AT_FIVE + s] for s in range(TOP_SLOTS)]

    early = []
    if fresh:
        picks, made = refs[3], refs[4]
        early.append(copies.start(blocks_in, picks))
        blocks = made
    else:
        blocks, all_sums, row = refs[3], refs[4], refs[5]
        early.append(copies.start(blocks_in, blocks))
        arrive_sums = copies.start(message_in.at[:, RHS : RHS + 8, :], all_sums)
    for s, n in enumerate(fives):
        early.append(copies.start(message_in.at[pl.ds(4 * n, 4)], nodes.at[4 * s : 4 * s + 4]))
    for s, n in enumerate(fours):
        early.append(
            copies.start(message_in.at[pl.ds(2 * n, 2)], nodes.at[16 + 2 * s : 18 + 2 * s])
        )
    for s, n in enumerate(threes):
        early.append(copies.start(message_in.at[pl.ds(n, 1)], nodes.at[24 + s : 25 + s]))
    if fresh:
        early.append(copies.start(message_in.at[pl.ds(4 * node_five, 4)], nodes.at[26:30]))
    arrive = []
    for s, n in enumerate(fives):
        arrive.append(copies.start(up_top_in.at[pl.ds(2 * n, 2)], weights.at[3 * s : 3 * s + 2]))
        arrive.append(
            copies.start(
                up_top_in.at[pl.ds(NODES_FOUR + n, 1)], weights.at[3 * s + 2 : 3 * s + 3]
            )
        )
    for s, n in enumerate(fours + [node_four, NODES_FOUR + node_five]):
        arrive.append(copies.start(up_top_in.at[pl.ds(n, 1)], weights.at[12 + s : 13 + s]))
    arrive += [copies.start(source, target) for source, target in zip(sources, held)]
    interp, one, two, three, field, near_part = held[:6]
    wait_all(early)

    def pair_of(at, get):
        return jnp.concatenate([get(at), get(at + 1)], 1)

    if fresh:

        def base(at):
            return parts_of(nodes[at, RHS : RHS + DIMS, :])

        def four(at, n):
            return pick(pair_of(at, base), picks[pl.ds(n, 1), :])

        def five(at, n):
            both = jnp.concatenate([four(at, 2 * n), four(at + 2, 2 * n + 1)], 1)
            return pick(both, picks[pl.ds(NODES_FOUR + n, 1), :])

        def block(slot, own_left, other, differs):
            right = operands(joined(other))[1]
            made[slot] = jnp.exp2(mm(right.T, own_left)) * jnp.where(differs, 1.0, 0.0)

        own = operands(nodes[26 + dev % 4, RHS : RHS + DIMS, :])[0]
        for s, n in enumerate(threes):
            block(s, own, base(24 + s), n != dev)
        own = operands(joined(four(26 + 2 * (node_four % 2), node_four)))[0]
        for s, n in enumerate(fours):
            block(2 + s, own, four(16 + 2 * s, n), n != node_four)
        own = operands(joined(five(26, node_five)))[0]
        for s, n in enumerate(fives):
            block(6 + s, own, five(4 * s, n), n != node_five)
        leave = [copies.start(made, blocks_out)]
    else:
        leave = []

    def charge(at):
        return nodes[at, 0:RHS, :]

    field_three = jnp.zeros((RHS, RANK), F)
    for s in range(2):
        field_three = field_three + dot_split(charge(24 + s), blocks[s])
    wait_all(arrive)
    field_five = jnp.zeros((RHS, RANK), F)
    for s in range(TOP_SLOTS):
        lower = dot_split(pair_of(4 * s, charge), weights[3 * s])
        upper = dot_split(pair_of(4 * s + 2, charge), weights[3 * s + 1])
        q = dot_split(jnp.concatenate([lower, upper], 1), weights[3 * s + 2])
        field_five = field_five + dot_split(q, blocks[6 + s])
    field_four = jnp.zeros((RHS, RANK), F)
    for s in range(TOP_SLOTS):
        q = dot_split(pair_of(16 + 2 * s, charge), weights[12 + s])
        field_four = field_four + dot_split(q, blocks[2 + s])

    def half(at, side):
        return weights[at, pl.ds(pl.multiple_of(side * RANK, RANK), RANK), :]

    field_four = field_four + dot_split(field_five, half(17, node_four % 2), NT)
    level = [field_three + dot_split(field_four, half(16, dev % 2), NT)]
    for ref in (three, two, one):
        spread = [dot_split(h, ref[n], NT) for n, h in enumerate(level)]
        level = [s[:, side * RANK : (side + 1) * RANK] for s in spread for side in range(2)]
    for a in range(LEAVES_HERE):
        far = dot_split(level[a], interp[a], NT)
        image[:, cols(a)] = RIDGE_TERM * field[:, cols(a)] + near_part[:, cols(a)] + far
    leave.append(copies.start(image, image_out))
    if fresh:
        message = refs[5]
        charges = climb(image, interp, (one, two, three))
        sums = row_of_sums([field[...] * field[...], field[...] * image[...]])
        block = jnp.concatenate([charges, sums, jnp.zeros((7, RANK), F)], 0)
        message[...] = jnp.broadcast_to(block[None], message.shape)
        leave += send_copies(copies, message, message_out)
    else:
        wait_all([arrive_sums])
        base_field = held[6]
        all_sums[0] = jnp.sum(all_sums[...], 0)
        step = first_step(all_sums[0])
        residual = base_field[...] - step * field[...]
        moved = field[...] - step * image[...]
        sums = row_of_sums(
            [residual * residual, residual * moved, base_field[...] * moved, residual * field[...]]
        )
        row[...] = jnp.broadcast_to(sums, row.shape)
        leave.append(copies.start(row, rows_out))
        leave.append(copies.start(all_sums.at[0], sums_out))
    wait_all(leave)


def down(fresh, ids, message, blocks, up_top, *sources):
    made = shape((2 + 2 * TOP_SLOTS, RANK, RANK))
    rows = message.shape[1]
    scratch = scratch_for(sources) + [
        pltpu.VMEM((18, 2 * RANK, RANK), F),
        pltpu.VMEM((30, rows, RANK), F),
        pltpu.VMEM((RHS, WIDTH), F),
    ]
    if fresh:
        out = [shape((RHS, WIDTH)), shape((DEVICES, RHS + 8, RANK)), made]
        scratch += [
            pltpu.VMEM(blocks.shape, jnp.int32),
            pltpu.VMEM(made.shape, F),
            pltpu.VMEM((16, RHS + 8, RANK), F),
        ]
    else:
        out = [shape((RHS, WIDTH)), shape((DEVICES, RANK)), shape((8, RANK))]
        scratch += [
            pltpu.VMEM(made.shape, F),
            pltpu.VMEM((DEVICES, 8, RANK), F),
            pltpu.VMEM((DEVICES, RANK), F),
        ]
    return call(
        functools.partial(down_kernel, fresh),
        "down_first" if fresh else "down_second",
        out,
        ids,
        [message, blocks, up_top, *sources],
        scratch,
        10**9,
    )


def finish_kernel(*refs):
    inputs, (solution_out, residual_out) = refs[:5], refs[5:7]
    held, (solution_held, residual_held, semaphores) = refs[7:12], refs[12:]
    copies = Copies(semaphores)
    wait_all([copies.start(source, target) for source, target in zip(inputs, held)])
    rows_ref, sums_ref, base_ref, image_ref, second_ref = held
    before = columns(sums_ref[...])
    rows = jnp.sum(rows_ref[...], 0, keepdims=True)
    after = columns(jnp.broadcast_to(rows, (8, RANK)))
    norm, curvature = before[0:RHS], before[RHS : 2 * RHS]
    step = norm / curvature
    norm_next, rm, bm, ri = [after[q * RHS : (q + 1) * RHS] for q in range(4)]
    turn = norm_next / norm
    second_curvature = rm + turn * (bm + ri + turn * curvature)
    second_step = norm_next / second_curvature
    base = base_ref[...]
    image = image_ref[...]
    residual = base - step * image
    direction = residual + turn * base
    moved = image - step * second_ref[...] + turn * image
    solution_held[...] = step * base + second_step * direction
    leave = [copies.start(solution_held, solution_out)]
    residual_held[...] = residual - second_step * moved
    leave.append(copies.start(residual_held, residual_out))
    wait_all(leave)


def finish(*inputs):
    out = [shape((RHS, WIDTH))] * 2
    return call(finish_kernel, "finish", out, None, inputs, scratch_for(inputs) + scratch_for(out), 10**6)


def beside(value):
    partner = [(i, i ^ 1) for i in range(DEVICES)]
    forward = [(i, i + 1) for i in range(1, DEVICES - 1, 2)]
    other = forward + [(target, source) for source, target in forward]
    return lax.ppermute(value, AXES, partner), lax.ppermute(value, AXES, other)


def everyone(copies):
    return lax.all_to_all(copies, AXES, 0, 0, tiled=True)


def local(
    points,
    right_side,
    interp,
    leaf_skel,
    up_one,
    skel_one,
    up_two,
    skel_two,
    up_three,
    skel_three,
    up_top,
    skel_top,
    near_list,
    far_three,
    far_top,
):
    device = lax.axis_index(AXES).astype(jnp.int32)
    fours = lax.dynamic_index_in_dim(far_top, device // 2, 0, False)
    fives = lax.dynamic_index_in_dim(far_top, NODES_FOUR + device // 4, 0, False) - NODES_FOUR
    ids = jnp.concatenate(
        [device[None], far_three[0], fours, fives, jnp.zeros((5,), jnp.int32), near_list.reshape(-1)]
    )
    weights = (interp, up_one, up_two, up_three)
    message, halo = first(
        points, right_side, weights, (leaf_skel, skel_one, skel_two, skel_three)
    )
    partner, other = beside(halo)
    message = everyone(message)
    part, right, left = near(True, ids, points, right_side, partner, other)
    image, own_message, blocks = down(
        True, ids, message, skel_top, up_top, *weights, right_side, part
    )
    partner, other = beside(image)
    message = everyone(own_message)
    (part,) = near(False, ids, right, left, image, partner, other)
    second, rows, sums = down(
        False, ids, message, blocks, up_top, *weights, image, part, right_side
    )
    return tuple(finish(everyone(rows), sums, right_side, image, second))


def solution(mesh):
    both = ("leaf", "sub")
    placed = (
        P(None, both),
        P(None, both),
        P(both, None, None),
        P(both, None),
        P(both, None, None),
        P(both, None),
        P(both, None, None),
        P(both, None),
        P(both, None, None),
        P(both, None),
        P(),
        P(),
        P(both, None),
        P(both, None),
        P(),
    )
    return jax.shard_map(
        local,
        mesh=mesh,
        in_specs=placed,
        out_specs=(P(None, both), P(None, both)),
        check_vma=False,
    )
```

```python
import functools
import math

import jax
import jax.numpy as jnp
from jax import lax
from jax.experimental import pallas as pl
from jax.experimental.pallas import tpu as pltpu
from jax.sharding import PartitionSpec as P

LEAF = 512
DIMS = 32
RHS = 16
RANK = 128
LEAVES_HERE = 8
SLOTS = 12
WIDTH = LEAVES_HERE * LEAF
DEVICES = 128
NODES_FOUR = 64
TOP_SLOTS = 4
AT_THREE, AT_FOUR, AT_FIVE, AT_NEAR = 1, 3, 7, 16

RIDGE_TERM = 12.0
COORD_SCALE = math.sqrt(2.0 * math.log2(math.e) / 24.0)

AXES = ("leaf", "sub")
BF = jnp.bfloat16
F = jnp.float32
NN = (((1,), (0,)), ((), ()))
NT = (((1,), (1,)), ((), ()))
SMEM = pl.BlockSpec(memory_space=pltpu.SMEM)
ANY = pl.BlockSpec(memory_space=pl.ANY)


def shape(dims, dtype=F):
    return jax.ShapeDtypeStruct(dims, dtype)


def mm(a, b, dims=NN):
    return lax.dot_general(a, b, dims, preferred_element_type=F)


def split_two(x):
    high = x.astype(BF)
    return high, (x - high.astype(F)).astype(BF)


def split_three(x):
    high = x.astype(BF)
    rest = x - high.astype(F)
    mid = rest.astype(BF)
    return high, mid, (rest - mid.astype(F)).astype(BF)


def dot_split(a, w, dims=NN):
    ah, am = split_two(a)
    wh, wm = split_two(w)
    both = mm(jnp.concatenate([ah, am], 0), wh, dims)
    return both[:RHS] + both[RHS:] + mm(ah, wm, dims)


def operands(y):
    n = y.shape[1]
    h, m, l = split_three(y)
    half = 0.5 * jnp.sum(y * y, 0, keepdims=True)
    parts = [p.astype(F) for p in split_three(half)]
    one = [jnp.ones((1, n), F)] * 3
    pad = [jnp.zeros((10, n), F)]
    tail_left = jnp.concatenate(parts + one + pad, 0).astype(BF)
    tail_right = jnp.concatenate([-p for p in one + parts] + pad, 0).astype(BF)
    zero = jnp.zeros((48, n), BF)
    left = jnp.concatenate([h, h, m, h, l, m, tail_left, zero], 0)
    right = jnp.concatenate([h, m, h, l, h, m, tail_right, zero], 0)
    return left, right


def pick(parts, chosen):
    n = parts.shape[1]
    rows = lax.broadcasted_iota(jnp.int32, (n, RANK), 0)
    hot = jnp.where(rows == chosen, 1.0, 0.0).astype(BF)
    return mm(parts, hot).astype(BF)


def joined(parts):
    return parts[0:32].astype(F) + parts[32:64].astype(F) + parts[64:96].astype(F)


def parts_of(y):
    return jnp.concatenate(split_three(y), 0)


class Copies:
    def __init__(self, semaphores):
        self.semaphores = semaphores
        self.used = 0

    def start(self, source, target):
        copy = pltpu.make_async_copy(source, target, self.semaphores.at[self.used])
        self.used += 1
        copy.start()
        return copy


def wait_all(copies):
    for copy in copies:
        copy.wait()


def call(kernel, name, out, ids, inputs, scratch, flops, transcendentals=0):
    operands_given = ([ids] if ids is not None else []) + list(inputs)
    return pl.pallas_call(
        kernel,
        out_shape=out,
        in_specs=([SMEM] if ids is not None else []) + [ANY] * len(inputs),
        out_specs=[ANY] * len(out),
        scratch_shapes=scratch + [pltpu.SemaphoreType.DMA((48,))],
        compiler_params=pltpu.CompilerParams(vmem_limit_bytes=63 << 20),
        cost_estimate=pl.CostEstimate(
            flops=flops, bytes_accessed=6 << 20, transcendentals=transcendentals
        ),
        name=name,
    )(*operands_given)


def scratch_for(arrays):
    return [pltpu.VMEM(a.shape, a.dtype) for a in arrays]


def cols(a):
    return slice(a * LEAF, (a + 1) * LEAF)


def row_of_sums(products):
    folded = []
    for value in products:
        piece = value[:, 0:RANK]
        for t in range(1, WIDTH // RANK):
            piece = piece + value[:, t * RANK : (t + 1) * RANK]
        folded.append(piece)
    rest = RANK - RHS * len(folded)
    stacked = jnp.concatenate(folded + [jnp.zeros((rest, RANK), F)], 0)
    return jnp.sum(stacked.T, 0, keepdims=True)


def climb(field, interp, transfers):
    level = [dot_split(field[:, cols(a)], interp[a]) for a in range(LEAVES_HERE)]
    for ref in transfers:
        level = [
            dot_split(jnp.concatenate([level[2 * n], level[2 * n + 1]], 1), ref[n])
            for n in range(len(level) // 2)
        ]
    return level[0]


def first_kernel(*refs):
    inputs, message_out = refs[:10], refs[10]
    held, (message, semaphores) = refs[11:21], refs[21:]
    copies = Copies(semaphores)
    arrive = [copies.start(source, target) for source, target in zip(inputs, held)]
    points, field, interp, one, two, three, leaf_pick, one_pick, two_pick, three_pick = held
    wait_all(arrive[0:2])
    wait_all(arrive[6:])
    level = [
        pick(parts_of(points[:, cols(a)] * COORD_SCALE), leaf_pick[a : a + 1, :])
        for a in range(LEAVES_HERE)
    ]
    for ref in (one_pick, two_pick, three_pick):
        level = [
            pick(jnp.concatenate([level[2 * n], level[2 * n + 1]], 1), ref[n : n + 1, :])
            for n in range(len(level) // 2)
        ]
    wait_all(arrive[2:6])
    charges = climb(field, interp, (one, two, three))
    block = jnp.concatenate([charges, joined(level[0])], 0)
    message[...] = jnp.broadcast_to(block[None], message.shape)
    wait_all(send_copies(copies, message, message_out))


def send_copies(copies, message, message_out):
    count = message.shape[0]
    return [
        copies.start(message, message_out.at[t * count : (t + 1) * count])
        for t in range(DEVICES // count)
    ]


def first(points, right_side, weights, picks):
    inputs = [points, right_side, *weights, *picks]
    return call(
        first_kernel,
        "first_up",
        [shape((DEVICES, RHS + DIMS, RANK))],
        None,
        inputs,
        scratch_for(inputs) + [pltpu.VMEM((16, RHS + DIMS, RANK), F)],
        10**9,
    )


def near_kernel(fresh, *refs):
    if fresh:
        ids_ref, points_in, field_in, partner_in, other_in, beside_in = refs[0:5] + (refs[5:7],)
        part_out, right_out, left_out = refs[7:10]
        points, field, partner, other = refs[10:14]
        beside_points = refs[14:16]
    else:
        ids_ref, right_in, left_in, field_in, partner_in, other_in, part_out = refs[:7]
        field, partner, other = refs[7:10]
    right, left, total, values, ea, eb, part, targets, origins, semaphores = refs[-10:]
    copies = Copies(semaphores)
    arrive_field = copies.start(field_in, field)
    if fresh:
        arrive_own = [copies.start(points_in, points)]
    else:
        arrive_own = [
            copies.start(left_in, left),
            copies.start(right_in.at[0:LEAVES_HERE], right.at[0:LEAVES_HERE]),
        ]
    arrive_beside = [copies.start(partner_in, partner), copies.start(other_in, other)]
    if fresh:
        arrive_beside += [copies.start(*pair) for pair in zip(beside_in, beside_points)]
    else:
        arrive_beside.append(
            copies.start(
                right_in.at[LEAVES_HERE : 3 * LEAVES_HERE], right.at[LEAVES_HERE : 3 * LEAVES_HERE]
            )
        )
    first = ids_ref[0] * LEAVES_HERE
    empty = 3 * LEAVES_HERE
    beside_at = 128
    odd = ids_ref[0] % 2 == 1
    shift_low = jnp.where(odd, 2 * LEAVES_HERE, 3 * LEAVES_HERE)
    shift_high = jnp.where(odd, LEAVES_HERE, 0)

    def collect(a, counts):
        n, m = counts
        targets[n] = a
        origins[n] = a
        n = n + 1
        for slot in range(SLOTS):
            place = ids_ref[AT_NEAR + a * SLOTS + slot] - first
            inside = (place >= 0) & (place < LEAVES_HERE)
            targets[n] = a
            origins[n] = place
            n = n + (inside & (place != a)).astype(jnp.int32)
            targets[m] = a
            origins[m] = place + jnp.where(place < 0, shift_low, shift_high)
            m = m + jnp.logical_not(inside).astype(jnp.int32)
        return n, m

    own_end, beside_end = lax.fori_loop(
        0, LEAVES_HERE, collect, (jnp.int32(0), jnp.int32(beside_at))
    )
    for end in (own_end, beside_end):
        for extra in range(4):
            targets[end + extra] = 0
            origins[end + extra] = empty

    def take_values(source, at):
        for a in range(LEAVES_HERE):
            values[at + a] = jnp.concatenate(split_three(source[:, cols(a)]), 0)

    def exponent(t):
        origin = origins[t]
        return mm(right[jnp.where(origin == empty, 0, origin)], left[targets[t]])

    def add(t, e):
        a = targets[t]
        v = values[origins[t]]
        block = jnp.exp2(e)
        upper = block.astype(BF)
        lower = (block - upper.astype(F)).astype(BF)
        total[a, 0:32] += mm(v[:32], upper)
        total[a, 0:16] += mm(v[:16], lower)

    def run(start, end):
        ea[...] = exponent(start)

        def pair(t):
            eb[...] = exponent(t + 1)
            add(t, ea[...])
            ea[...] = exponent(t + 2)
            add(t + 1, eb[...])

        def four(p, carry):
            pair(start + 4 * p)
            pair(start + 4 * p + 2)
            return carry

        def two(p, carry):
            pair(middle + 2 * p)
            return carry

        fours = (end - start) // 4
        middle = start + 4 * fours
        lax.fori_loop(0, fours, four, 0)
        lax.fori_loop(0, (end - middle + 1) // 2, two, 0)

    total[...] = jnp.zeros_like(total)
    values[empty] = jnp.zeros((3 * RHS, LEAF), BF)
    wait_all([arrive_field])
    take_values(field, 0)
    wait_all(arrive_own)
    leave = []
    if fresh:
        for a in range(LEAVES_HERE):
            left_part, right_part = operands(points[:, cols(a)] * COORD_SCALE)
            left[a] = left_part
            right[a] = right_part.T
        leave.append(copies.start(left, left_out))
        leave.append(copies.start(right.at[0:LEAVES_HERE], right_out.at[0:LEAVES_HERE]))
    run(0, own_end)
    wait_all(arrive_beside)
    take_values(partner, LEAVES_HERE)
    take_values(other, 2 * LEAVES_HERE)
    if fresh:
        for side, source in enumerate(beside_points):
            for a in range(LEAVES_HERE):
                y = source[:, cols(a)] * COORD_SCALE
                right[(side + 1) * LEAVES_HERE + a] = operands(y)[1].T
        beside = slice(LEAVES_HERE, 3 * LEAVES_HERE)
        leave.append(copies.start(right.at[beside], right_out.at[beside]))
    run(beside_at, beside_end)
    for a in range(LEAVES_HERE):
        part[:, cols(a)] = total[a, 0:16] + total[a, 16:32]
    leave.append(copies.start(part, part_out))
    wait_all(leave)


def near(fresh, ids, *inputs):
    right = shape((3 * LEAVES_HERE, LEAF, 256), BF)
    left = shape((LEAVES_HERE, 256, LEAF), BF)
    held = inputs if fresh else inputs[2:]
    return call(
        functools.partial(near_kernel, fresh),
        "near_first" if fresh else "near_second",
        [shape((RHS, WIDTH))] + ([right, left] if fresh else []),
        ids,
        inputs,
        scratch_for(held)
        + scratch_for([right, left])
        + [
            pltpu.VMEM((LEAVES_HERE, 32, LEAF), F),
            pltpu.VMEM((3 * LEAVES_HERE + 1, 3 * RHS, LEAF), BF),
            pltpu.VMEM((LEAF, LEAF), F),
            pltpu.VMEM((LEAF, LEAF), F),
            pltpu.VMEM((RHS, WIDTH), F),
            pltpu.SMEM((256,), jnp.int32),
            pltpu.SMEM((256,), jnp.int32),
        ],
        40 * 10**9,
        50 * LEAF * LEAF,
    )


def first_step(row_block):
    sums = columns(row_block)
    return sums[0:RHS] / sums[RHS : 2 * RHS]


def columns(row_block):
    return row_block.T[:, 0:1]


def down_kernel(fresh, *refs):
    ids_ref, message_in, blocks_in, up_top_in = refs[:4]
    if fresh:
        sources, (image_out, message_out, blocks_out) = refs[4:10], refs[10:13]
        refs = refs[13:]
    else:
        sources, (image_out, rows_out, sums_out) = refs[4:11], refs[11:14]
        refs = refs[14:]
    held, refs = refs[: len(sources)], refs[len(sources) :]
    weights, nodes, image, semaphores = refs[0], refs[1], refs[2], refs[-1]
    copies = Copies(semaphores)
    dev = ids_ref[0]
    node_four = dev // 2
    node_five = dev // 4
    threes = [ids_ref[AT_THREE + s] for s in range(2)]
    fours = [ids_ref[AT_FOUR + s] for s in range(TOP_SLOTS)]
    fives = [ids_ref[AT_FIVE + s] for s in range(TOP_SLOTS)]

    early = []
    if fresh:
        picks, made = refs[3], refs[4]
        early.append(copies.start(blocks_in, picks))
        blocks = made
    else:
        blocks, all_sums, row = refs[3], refs[4], refs[5]
        early.append(copies.start(blocks_in, blocks))
        arrive_sums = copies.start(message_in.at[:, RHS : RHS + 8, :], all_sums)
    for s, n in enumerate(fives):
        early.append(copies.start(message_in.at[pl.ds(4 * n, 4)], nodes.at[4 * s : 4 * s + 4]))
    for s, n in enumerate(fours):
        early.append(
            copies.start(message_in.at[pl.ds(2 * n, 2)], nodes.at[16 + 2 * s : 18 + 2 * s])
        )
    for s, n in enumerate(threes):
        early.append(copies.start(message_in.at[pl.ds(n, 1)], nodes.at[24 + s : 25 + s]))
    if fresh:
        early.append(copies.start(message_in.at[pl.ds(4 * node_five, 4)], nodes.at[26:30]))
    arrive = []
    for s, n in enumerate(fives):
        arrive.append(copies.start(up_top_in.at[pl.ds(2 * n, 2)], weights.at[3 * s : 3 * s + 2]))
        arrive.append(
            copies.start(
                up_top_in.at[pl.ds(NODES_FOUR + n, 1)], weights.at[3 * s + 2 : 3 * s + 3]
            )
        )
    for s, n in enumerate(fours + [node_four, NODES_FOUR + node_five]):
        arrive.append(copies.start(up_top_in.at[pl.ds(n, 1)], weights.at[12 + s : 13 + s]))
    arrive += [copies.start(source, target) for source, target in zip(sources, held)]
    interp, one, two, three, field, near_part = held[:6]
    wait_all(early)

    def pair_of(at, get):
        return jnp.concatenate([get(at), get(at + 1)], 1)

    if fresh:

        def base(at):
            return parts_of(nodes[at, RHS : RHS + DIMS, :])

        def four(at, n):
            return pick(pair_of(at, base), picks[pl.ds(n, 1), :])

        def five(at, n):
            both = jnp.concatenate([four(at, 2 * n), four(at + 2, 2 * n + 1)], 1)
            return pick(both, picks[pl.ds(NODES_FOUR + n, 1), :])

        def block(slot, own_left, other, differs):
            right = operands(joined(other))[1]
            made[slot] = jnp.exp2(mm(right.T, own_left)) * jnp.where(differs, 1.0, 0.0)

        own = operands(nodes[26 + dev % 4, RHS : RHS + DIMS, :])[0]
        for s, n in enumerate(threes):
            block(s, own, base(24 + s), n != dev)
        own = operands(joined(four(26 + 2 * (node_four % 2), node_four)))[0]
        for s, n in enumerate(fours):
            block(2 + s, own, four(16 + 2 * s, n), n != node_four)
        own = operands(joined(five(26, node_five)))[0]
        for s, n in enumerate(fives):
            block(6 + s, own, five(4 * s, n), n != node_five)
        leave = [copies.start(made, blocks_out)]
    else:
        leave = []

    def charge(at):
        return nodes[at, 0:RHS, :]

    field_three = jnp.zeros((RHS, RANK), F)
    for s in range(2):
        field_three = field_three + dot_split(charge(24 + s), blocks[s])
    wait_all(arrive)
    field_five = jnp.zeros((RHS, RANK), F)
    for s in range(TOP_SLOTS):
        lower = dot_split(pair_of(4 * s, charge), weights[3 * s])
        upper = dot_split(pair_of(4 * s + 2, charge), weights[3 * s + 1])
        q = dot_split(jnp.concatenate([lower, upper], 1), weights[3 * s + 2])
        field_five = field_five + dot_split(q, blocks[6 + s])
    field_four = jnp.zeros((RHS, RANK), F)
    for s in range(TOP_SLOTS):
        q = dot_split(pair_of(16 + 2 * s, charge), weights[12 + s])
        field_four = field_four + dot_split(q, blocks[2 + s])

    def half(at, side):
        return weights[at, pl.ds(pl.multiple_of(side * RANK, RANK), RANK), :]

    field_four = field_four + dot_split(field_five, half(17, node_four % 2), NT)
    level = [field_three + dot_split(field_four, half(16, dev % 2), NT)]
    for ref in (three, two, one):
        spread = [dot_split(h, ref[n], NT) for n, h in enumerate(level)]
        level = [s[:, side * RANK : (side + 1) * RANK] for s in spread for side in range(2)]
    for a in range(LEAVES_HERE):
        far = dot_split(level[a], interp[a], NT)
        image[:, cols(a)] = RIDGE_TERM * field[:, cols(a)] + near_part[:, cols(a)] + far
    leave.append(copies.start(image, image_out))
    if fresh:
        message = refs[5]
        charges = climb(image, interp, (one, two, three))
        sums = row_of_sums([field[...] * field[...], field[...] * image[...]])
        block = jnp.concatenate([charges, sums, jnp.zeros((7, RANK), F)], 0)
        message[...] = jnp.broadcast_to(block[None], message.shape)
        leave += send_copies(copies, message, message_out)
    else:
        wait_all([arrive_sums])
        base_field = held[6]
        all_sums[0] = jnp.sum(all_sums[...], 0)
        step = first_step(all_sums[0])
        residual = base_field[...] - step * field[...]
        moved = field[...] - step * image[...]
        sums = row_of_sums(
            [residual * residual, residual * moved, base_field[...] * moved, residual * field[...]]
        )
        row[...] = jnp.broadcast_to(sums, row.shape)
        leave.append(copies.start(row, rows_out))
        leave.append(copies.start(all_sums.at[0], sums_out))
    wait_all(leave)


def down(fresh, ids, message, blocks, up_top, *sources):
    made = shape((2 + 2 * TOP_SLOTS, RANK, RANK))
    rows = message.shape[1]
    scratch = scratch_for(sources) + [
        pltpu.VMEM((18, 2 * RANK, RANK), F),
        pltpu.VMEM((30, rows, RANK), F),
        pltpu.VMEM((RHS, WIDTH), F),
    ]
    if fresh:
        out = [shape((RHS, WIDTH)), shape((DEVICES, RHS + 8, RANK)), made]
        scratch += [
            pltpu.VMEM(blocks.shape, jnp.int32),
            pltpu.VMEM(made.shape, F),
            pltpu.VMEM((16, RHS + 8, RANK), F),
        ]
    else:
        out = [shape((RHS, WIDTH)), shape((DEVICES, RANK)), shape((8, RANK))]
        scratch += [
            pltpu.VMEM(made.shape, F),
            pltpu.VMEM((DEVICES, 8, RANK), F),
            pltpu.VMEM((DEVICES, RANK), F),
        ]
    return call(
        functools.partial(down_kernel, fresh),
        "down_first" if fresh else "down_second",
        out,
        ids,
        [message, blocks, up_top, *sources],
        scratch,
        10**9,
    )


def finish_kernel(*refs):
    inputs, (solution_out, residual_out) = refs[:5], refs[5:7]
    held, (solution_held, residual_held, semaphores) = refs[7:12], refs[12:]
    copies = Copies(semaphores)
    wait_all([copies.start(source, target) for source, target in zip(inputs, held)])
    rows_ref, sums_ref, base_ref, image_ref, second_ref = held
    before = columns(sums_ref[...])
    rows = jnp.sum(rows_ref[...], 0, keepdims=True)
    after = columns(jnp.broadcast_to(rows, (8, RANK)))
    norm, curvature = before[0:RHS], before[RHS : 2 * RHS]
    step = norm / curvature
    norm_next, rm, bm, ri = [after[q * RHS : (q + 1) * RHS] for q in range(4)]
    turn = norm_next / norm
    second_curvature = rm + turn * (bm + ri + turn * curvature)
    second_step = norm_next / second_curvature
    base = base_ref[...]
    image = image_ref[...]
    residual = base - step * image
    direction = residual + turn * base
    moved = image - step * second_ref[...] + turn * image
    solution_held[...] = step * base + second_step * direction
    leave = [copies.start(solution_held, solution_out)]
    residual_held[...] = residual - second_step * moved
    leave.append(copies.start(residual_held, residual_out))
    wait_all(leave)


def finish(*inputs):
    out = [shape((RHS, WIDTH))] * 2
    return call(finish_kernel, "finish", out, None, inputs, scratch_for(inputs) + scratch_for(out), 10**6)


def beside(value):
    partner = [(i, i ^ 1) for i in range(DEVICES)]
    forward = [(i, i + 1) for i in range(1, DEVICES - 1, 2)]
    other = forward + [(target, source) for source, target in forward]
    return lax.ppermute(value, AXES, partner), lax.ppermute(value, AXES, other)


def everyone(copies):
    return lax.all_to_all(copies, AXES, 0, 0, tiled=True)


def local(
    points,
    right_side,
    interp,
    leaf_skel,
    up_one,
    skel_one,
    up_two,
    skel_two,
    up_three,
    skel_three,
    up_top,
    skel_top,
    near_list,
    far_three,
    far_top,
):
    device = lax.axis_index(AXES).astype(jnp.int32)
    fours = lax.dynamic_index_in_dim(far_top, device // 2, 0, False)
    fives = lax.dynamic_index_in_dim(far_top, NODES_FOUR + device // 4, 0, False) - NODES_FOUR
    ids = jnp.concatenate(
        [device[None], far_three[0], fours, fives, jnp.zeros((5,), jnp.int32), near_list.reshape(-1)]
    )
    weights = (interp, up_one, up_two, up_three)
    (message,) = first(points, right_side, weights, (leaf_skel, skel_one, skel_two, skel_three))
    message = everyone(message)
    part, right, left = near(
        True, ids, points, right_side, *beside(right_side), *beside(points)
    )
    image, own_message, blocks = down(
        True, ids, message, skel_top, up_top, *weights, right_side, part
    )
    partner, other = beside(image)
    message = everyone(own_message)
    (part,) = near(False, ids, right, left, image, partner, other)
    second, rows, sums = down(
        False, ids, message, blocks, up_top, *weights, image, part, right_side
    )
    return tuple(finish(everyone(rows), sums, right_side, image, second))


def solution(mesh):
    both = ("leaf", "sub")
    placed = (
        P(None, both),
        P(None, both),
        P(both, None, None),
        P(both, None),
        P(both, None, None),
        P(both, None),
        P(both, None, None),
        P(both, None),
        P(both, None, None),
        P(both, None),
        P(),
        P(),
        P(both, None),
        P(both, None),
        P(),
    )
    return jax.shard_map(
        local,
        mesh=mesh,
        in_specs=placed,
        out_specs=(P(None, both), P(None, both)),
        check_vma=False,
    )
```

```python
import functools
import math

import jax
import jax.numpy as jnp
from jax import lax
from jax.experimental import pallas as pl
from jax.experimental.pallas import tpu as pltpu
from jax.sharding import PartitionSpec as P

LEAF = 512
DIMS = 32
RHS = 16
RANK = 128
LEAVES_HERE = 8
SLOTS = 12
WIDTH = LEAVES_HERE * LEAF
DEVICES = 128
NODES_FOUR = 64
TOP_SLOTS = 4
AT_THREE, AT_FOUR, AT_FIVE, AT_NEAR = 1, 3, 7, 16

RIDGE_TERM = 12.0
COORD_SCALE = math.sqrt(2.0 * math.log2(math.e) / 24.0)

AXES = ("leaf", "sub")
BF = jnp.bfloat16
F = jnp.float32
NN = (((1,), (0,)), ((), ()))
NT = (((1,), (1,)), ((), ()))
SMEM = pl.BlockSpec(memory_space=pltpu.SMEM)
ANY = pl.BlockSpec(memory_space=pl.ANY)


def shape(dims, dtype=F):
    return jax.ShapeDtypeStruct(dims, dtype)


def mm(a, b, dims=NN):
    return lax.dot_general(a, b, dims, preferred_element_type=F)


def split_two(x):
    high = x.astype(BF)
    return high, (x - high.astype(F)).astype(BF)


def split_three(x):
    high = x.astype(BF)
    rest = x - high.astype(F)
    mid = rest.astype(BF)
    return high, mid, (rest - mid.astype(F)).astype(BF)


def dot_split(a, w, dims=NN):
    ah, am = split_two(a)
    wh, wm = split_two(w)
    both = mm(jnp.concatenate([ah, am], 0), wh, dims)
    return both[:RHS] + both[RHS:] + mm(ah, wm, dims)


def operands(y):
    n = y.shape[1]
    h, m, l = split_three(y)
    half = 0.5 * jnp.sum(y * y, 0, keepdims=True)
    parts = [p.astype(F) for p in split_three(half)]
    one = [jnp.ones((1, n), F)] * 3
    pad = [jnp.zeros((10, n), F)]
    tail_left = jnp.concatenate(parts + one + pad, 0).astype(BF)
    tail_right = jnp.concatenate([-p for p in one + parts] + pad, 0).astype(BF)
    zero = jnp.zeros((48, n), BF)
    left = jnp.concatenate([h, h, m, h, l, m, tail_left, zero], 0)
    right = jnp.concatenate([h, m, h, l, h, m, tail_right, zero], 0)
    return left, right


def pick(parts, chosen):
    n = parts.shape[1]
    rows = lax.broadcasted_iota(jnp.int32, (n, RANK), 0)
    hot = jnp.where(rows == chosen, 1.0, 0.0).astype(BF)
    return mm(parts, hot).astype(BF)


def joined(parts):
    return parts[0:32].astype(F) + parts[32:64].astype(F) + parts[64:96].astype(F)


def parts_of(y):
    return jnp.concatenate(split_three(y), 0)


class Copies:
    def __init__(self, semaphores):
        self.semaphores = semaphores
        self.used = 0

    def start(self, source, target):
        copy = pltpu.make_async_copy(source, target, self.semaphores.at[self.used])
        self.used += 1
        copy.start()
        return copy


def wait_all(copies):
    for copy in copies:
        copy.wait()


def call(kernel, name, out, ids, inputs, scratch, flops, transcendentals=0):
    operands_given = ([ids] if ids is not None else []) + list(inputs)
    return pl.pallas_call(
        kernel,
        out_shape=out,
        in_specs=([SMEM] if ids is not None else []) + [ANY] * len(inputs),
        out_specs=[ANY] * len(out),
        scratch_shapes=scratch + [pltpu.SemaphoreType.DMA((48,))],
        compiler_params=pltpu.CompilerParams(vmem_limit_bytes=63 << 20),
        cost_estimate=pl.CostEstimate(
            flops=flops, bytes_accessed=6 << 20, transcendentals=transcendentals
        ),
        name=name,
    )(*operands_given)


def scratch_for(arrays):
    return [pltpu.VMEM(a.shape, a.dtype) for a in arrays]


def cols(a):
    return slice(a * LEAF, (a + 1) * LEAF)


def row_of_sums(products):
    folded = []
    for value in products:
        piece = value[:, 0:RANK]
        for t in range(1, WIDTH // RANK):
            piece = piece + value[:, t * RANK : (t + 1) * RANK]
        folded.append(piece)
    rest = RANK - RHS * len(folded)
    stacked = jnp.concatenate(folded + [jnp.zeros((rest, RANK), F)], 0)
    return jnp.sum(stacked.T, 0, keepdims=True)


def climb(field, interp, transfers):
    level = [dot_split(field[:, cols(a)], interp[a]) for a in range(LEAVES_HERE)]
    for ref in transfers:
        level = [
            dot_split(jnp.concatenate([level[2 * n], level[2 * n + 1]], 1), ref[n])
            for n in range(len(level) // 2)
        ]
    return level[0]


def first_kernel(*refs):
    inputs, message_out = refs[:10], refs[10]
    held, (message, semaphores) = refs[11:21], refs[21:]
    copies = Copies(semaphores)
    arrive = [copies.start(source, target) for source, target in zip(inputs, held)]
    points, field, interp, one, two, three, leaf_pick, one_pick, two_pick, three_pick = held
    wait_all(arrive[0:2])
    wait_all(arrive[6:])
    level = [
        pick(parts_of(points[:, cols(a)] * COORD_SCALE), leaf_pick[a : a + 1, :])
        for a in range(LEAVES_HERE)
    ]
    for ref in (one_pick, two_pick, three_pick):
        level = [
            pick(jnp.concatenate([level[2 * n], level[2 * n + 1]], 1), ref[n : n + 1, :])
            for n in range(len(level) // 2)
        ]
    message[:, RHS : RHS + DIMS, :] = jnp.broadcast_to(
        joined(level[0])[None], (message.shape[0], DIMS, RANK)
    )
    leave = send_copies(copies, message, message_out, slice(RHS, RHS + DIMS))
    wait_all(arrive[2:6])
    charges = climb(field, interp, (one, two, three))
    message[:, 0:RHS, :] = jnp.broadcast_to(charges[None], (message.shape[0], RHS, RANK))
    leave += send_copies(copies, message, message_out, slice(0, RHS))
    wait_all(leave)


def send_copies(copies, message, message_out, rows):
    count = message.shape[0]
    return [
        copies.start(message.at[:, rows], message_out.at[t * count : (t + 1) * count, rows])
        for t in range(DEVICES // count)
    ]


def halo_kernel(points_in, field_in, out, held, semaphores):
    copies = Copies(semaphores)
    wait_all(
        [
            copies.start(points_in, held.at[0:DIMS, :]),
            copies.start(field_in, held.at[DIMS : DIMS + RHS, :]),
        ]
    )
    wait_all([copies.start(held, out)])


def halo(points, right_side):
    out = shape((DIMS + RHS, WIDTH))
    return call(halo_kernel, "halo", [out], None, [points, right_side], scratch_for([out]), 1000)[0]


def first(points, right_side, weights, picks):
    inputs = [points, right_side, *weights, *picks]
    return call(
        first_kernel,
        "first_up",
        [shape((DEVICES, RHS + DIMS, RANK))],
        None,
        inputs,
        scratch_for(inputs) + [pltpu.VMEM((16, RHS + DIMS, RANK), F)],
        10**9,
    )


def near_kernel(fresh, *refs):
    if fresh:
        ids_ref, points_in, field_in, partner_in, other_in, part_out, right_out, left_out = refs[:8]
        points, field, partner, other = refs[8:12]
    else:
        ids_ref, right_in, left_in, field_in, partner_in, other_in, part_out = refs[:7]
        field, partner, other = refs[7:10]
    right, left, total, values, ea, eb, part, targets, origins, semaphores = refs[-10:]
    copies = Copies(semaphores)
    arrive_field = copies.start(field_in, field)
    if fresh:
        arrive_own = [copies.start(points_in, points)]
    else:
        arrive_own = [
            copies.start(left_in, left),
            copies.start(right_in.at[0:LEAVES_HERE], right.at[0:LEAVES_HERE]),
        ]
    arrive_beside = [copies.start(partner_in, partner), copies.start(other_in, other)]
    if not fresh:
        arrive_beside.append(
            copies.start(
                right_in.at[LEAVES_HERE : 3 * LEAVES_HERE], right.at[LEAVES_HERE : 3 * LEAVES_HERE]
            )
        )
    first = ids_ref[0] * LEAVES_HERE
    empty = 3 * LEAVES_HERE
    beside_at = 128
    odd = ids_ref[0] % 2 == 1
    shift_low = jnp.where(odd, 2 * LEAVES_HERE, 3 * LEAVES_HERE)
    shift_high = jnp.where(odd, LEAVES_HERE, 0)

    def collect(a, counts):
        n, m = counts
        targets[n] = a
        origins[n] = a
        n = n + 1
        for slot in range(SLOTS):
            place = ids_ref[AT_NEAR + a * SLOTS + slot] - first
            inside = (place >= 0) & (place < LEAVES_HERE)
            targets[n] = a
            origins[n] = place
            n = n + (inside & (place != a)).astype(jnp.int32)
            targets[m] = a
            origins[m] = place + jnp.where(place < 0, shift_low, shift_high)
            m = m + jnp.logical_not(inside).astype(jnp.int32)
        return n, m

    own_end, beside_end = lax.fori_loop(
        0, LEAVES_HERE, collect, (jnp.int32(0), jnp.int32(beside_at))
    )
    for end in (own_end, beside_end):
        for extra in range(4):
            targets[end + extra] = 0
            origins[end + extra] = empty

    def take_values(source, at):
        for a in range(LEAVES_HERE):
            values[at + a] = jnp.concatenate(split_three(source[source.shape[0] - RHS :, cols(a)]), 0)

    def exponent(t):
        origin = origins[t]
        return mm(right[jnp.where(origin == empty, 0, origin)], left[targets[t]])

    def add(t, e):
        a = targets[t]
        v = values[origins[t]]
        block = jnp.exp2(e)
        upper = block.astype(BF)
        lower = (block - upper.astype(F)).astype(BF)
        total[a, 0:32] += mm(v[:32], upper)
        total[a, 0:16] += mm(v[:16], lower)

    def run(start, end):
        ea[...] = exponent(start)

        def pair(t):
            eb[...] = exponent(t + 1)
            add(t, ea[...])
            ea[...] = exponent(t + 2)
            add(t + 1, eb[...])

        def eight(p, carry):
            for u in range(4):
                pair(start + 8 * p + 2 * u)
            return carry

        def two(p, carry):
            pair(middle + 2 * p)
            return carry

        eights = (end - start) // 8
        middle = start + 8 * eights
        lax.fori_loop(0, eights, eight, 0)
        lax.fori_loop(0, (end - middle + 1) // 2, two, 0)

    total[...] = jnp.zeros_like(total)
    values[empty] = jnp.zeros((3 * RHS, LEAF), BF)
    wait_all([arrive_field])
    take_values(field, 0)
    wait_all(arrive_own)
    leave = []
    if fresh:
        for a in range(LEAVES_HERE):
            left_part, right_part = operands(points[:, cols(a)] * COORD_SCALE)
            left[a] = left_part
            right[a] = right_part.T
        leave.append(copies.start(left, left_out))
        leave.append(copies.start(right.at[0:LEAVES_HERE], right_out.at[0:LEAVES_HERE]))
    run(0, own_end)
    wait_all(arrive_beside)
    take_values(partner, LEAVES_HERE)
    take_values(other, 2 * LEAVES_HERE)
    if fresh:
        for side, source in enumerate((partner, other)):
            for a in range(LEAVES_HERE):
                y = source[0:DIMS, cols(a)] * COORD_SCALE
                right[(side + 1) * LEAVES_HERE + a] = operands(y)[1].T
        beside = slice(LEAVES_HERE, 3 * LEAVES_HERE)
        leave.append(copies.start(right.at[beside], right_out.at[beside]))
    run(beside_at, beside_end)
    for a in range(LEAVES_HERE):
        part[:, cols(a)] = total[a, 0:16] + total[a, 16:32]
    leave.append(copies.start(part, part_out))
    wait_all(leave)


def near(fresh, ids, *inputs):
    right = shape((3 * LEAVES_HERE, LEAF, 256), BF)
    left = shape((LEAVES_HERE, 256, LEAF), BF)
    held = inputs if fresh else inputs[2:]
    return call(
        functools.partial(near_kernel, fresh),
        "near_first" if fresh else "near_second",
        [shape((RHS, WIDTH))] + ([right, left] if fresh else []),
        ids,
        inputs,
        scratch_for(held)
        + scratch_for([right, left])
        + [
            pltpu.VMEM((LEAVES_HERE, 32, LEAF), F),
            pltpu.VMEM((3 * LEAVES_HERE + 1, 3 * RHS, LEAF), BF),
            pltpu.VMEM((LEAF, LEAF), F),
            pltpu.VMEM((LEAF, LEAF), F),
            pltpu.VMEM((RHS, WIDTH), F),
            pltpu.SMEM((256,), jnp.int32),
            pltpu.SMEM((256,), jnp.int32),
        ],
        40 * 10**9,
        50 * LEAF * LEAF,
    )


def first_step(row_block):
    sums = columns(row_block)
    return sums[0:RHS] / sums[RHS : 2 * RHS]


def columns(row_block):
    return row_block.T[:, 0:1]


def down_kernel(fresh, *refs):
    ids_ref, message_in, blocks_in, up_top_in = refs[:4]
    if fresh:
        sources, (image_out, message_out, blocks_out) = refs[4:10], refs[10:13]
        refs = refs[13:]
    else:
        sources, (image_out, rows_out, sums_out) = refs[4:11], refs[11:14]
        refs = refs[14:]
    held, refs = refs[: len(sources)], refs[len(sources) :]
    weights, nodes, image, semaphores = refs[0], refs[1], refs[2], refs[-1]
    copies = Copies(semaphores)
    dev = ids_ref[0]
    node_four = dev // 2
    node_five = dev // 4
    threes = [ids_ref[AT_THREE + s] for s in range(2)]
    fours = [ids_ref[AT_FOUR + s] for s in range(TOP_SLOTS)]
    fives = [ids_ref[AT_FIVE + s] for s in range(TOP_SLOTS)]

    early = []
    if fresh:
        picks, made = refs[3], refs[4]
        early.append(copies.start(blocks_in, picks))
        blocks = made
    else:
        blocks, all_sums, row = refs[3], refs[4], refs[5]
        early.append(copies.start(blocks_in, blocks))
        arrive_sums = copies.start(message_in.at[:, RHS : RHS + 8, :], all_sums)
    for s, n in enumerate(fives):
        early.append(copies.start(message_in.at[pl.ds(4 * n, 4)], nodes.at[4 * s : 4 * s + 4]))
    for s, n in enumerate(fours):
        early.append(
            copies.start(message_in.at[pl.ds(2 * n, 2)], nodes.at[16 + 2 * s : 18 + 2 * s])
        )
    for s, n in enumerate(threes):
        early.append(copies.start(message_in.at[pl.ds(n, 1)], nodes.at[24 + s : 25 + s]))
    if fresh:
        early.append(copies.start(message_in.at[pl.ds(4 * node_five, 4)], nodes.at[26:30]))
    arrive = []
    for s, n in enumerate(fives):
        arrive.append(copies.start(up_top_in.at[pl.ds(2 * n, 2)], weights.at[3 * s : 3 * s + 2]))
        arrive.append(
            copies.start(
                up_top_in.at[pl.ds(NODES_FOUR + n, 1)], weights.at[3 * s + 2 : 3 * s + 3]
            )
        )
    for s, n in enumerate(fours + [node_four, NODES_FOUR + node_five]):
        arrive.append(copies.start(up_top_in.at[pl.ds(n, 1)], weights.at[12 + s : 13 + s]))
    arrive_held = [copies.start(source, target) for source, target in zip(sources, held)]
    interp, one, two, three, field, near_part = held[:6]
    wait_all(early)

    def pair_of(at, get):
        return jnp.concatenate([get(at), get(at + 1)], 1)

    if fresh:

        def base(at):
            return parts_of(nodes[at, RHS : RHS + DIMS, :])

        def four(at, n):
            return pick(pair_of(at, base), picks[pl.ds(n, 1), :])

        def five(at, n):
            both = jnp.concatenate([four(at, 2 * n), four(at + 2, 2 * n + 1)], 1)
            return pick(both, picks[pl.ds(NODES_FOUR + n, 1), :])

        def block(slot, own_left, other, differs):
            right = operands(joined(other))[1]
            made[slot] = jnp.exp2(mm(right.T, own_left)) * jnp.where(differs, 1.0, 0.0)

        own = operands(nodes[26 + dev % 4, RHS : RHS + DIMS, :])[0]
        for s, n in enumerate(threes):
            block(s, own, base(24 + s), n != dev)
        own = operands(joined(four(26 + 2 * (node_four % 2), node_four)))[0]
        for s, n in enumerate(fours):
            block(2 + s, own, four(16 + 2 * s, n), n != node_four)
        own = operands(joined(five(26, node_five)))[0]
        for s, n in enumerate(fives):
            block(6 + s, own, five(4 * s, n), n != node_five)
        leave = [copies.start(made, blocks_out)]
    else:
        leave = []

    def charge(at):
        return nodes[at, 0:RHS, :]

    field_three = jnp.zeros((RHS, RANK), F)
    for s in range(2):
        field_three = field_three + dot_split(charge(24 + s), blocks[s])
    wait_all(arrive)
    field_five = jnp.zeros((RHS, RANK), F)
    for s in range(TOP_SLOTS):
        lower = dot_split(pair_of(4 * s, charge), weights[3 * s])
        upper = dot_split(pair_of(4 * s + 2, charge), weights[3 * s + 1])
        q = dot_split(jnp.concatenate([lower, upper], 1), weights[3 * s + 2])
        field_five = field_five + dot_split(q, blocks[6 + s])
    field_four = jnp.zeros((RHS, RANK), F)
    for s in range(TOP_SLOTS):
        q = dot_split(pair_of(16 + 2 * s, charge), weights[12 + s])
        field_four = field_four + dot_split(q, blocks[2 + s])

    def half(at, side):
        return weights[at, pl.ds(pl.multiple_of(side * RANK, RANK), RANK), :]

    field_four = field_four + dot_split(field_five, half(17, node_four % 2), NT)
    level = [field_three + dot_split(field_four, half(16, dev % 2), NT)]
    wait_all(arrive_held)
    for ref in (three, two, one):
        spread = [dot_split(h, ref[n], NT) for n, h in enumerate(level)]
        level = [s[:, side * RANK : (side + 1) * RANK] for s in spread for side in range(2)]
    for a in range(LEAVES_HERE):
        far = dot_split(level[a], interp[a], NT)
        image[:, cols(a)] = RIDGE_TERM * field[:, cols(a)] + near_part[:, cols(a)] + far
    leave.append(copies.start(image, image_out))
    if fresh:
        message = refs[5]
        charges = climb(image, interp, (one, two, three))
        sums = row_of_sums([field[...] * field[...], field[...] * image[...]])
        block = jnp.concatenate([charges, sums, jnp.zeros((7, RANK), F)], 0)
        message[...] = jnp.broadcast_to(block[None], message.shape)
        leave += send_copies(copies, message, message_out, slice(0, RHS + 8))
    else:
        wait_all([arrive_sums])
        base_field = held[6]
        all_sums[0] = jnp.sum(all_sums[...], 0)
        step = first_step(all_sums[0])
        residual = base_field[...] - step * field[...]
        moved = field[...] - step * image[...]
        sums = row_of_sums(
            [residual * residual, residual * moved, base_field[...] * moved, residual * field[...]]
        )
        row[...] = jnp.broadcast_to(sums, row.shape)
        leave.append(copies.start(row, rows_out))
        leave.append(copies.start(all_sums.at[0], sums_out))
    wait_all(leave)


def down(fresh, ids, message, blocks, up_top, *sources):
    made = shape((2 + 2 * TOP_SLOTS, RANK, RANK))
    rows = message.shape[1]
    scratch = scratch_for(sources) + [
        pltpu.VMEM((18, 2 * RANK, RANK), F),
        pltpu.VMEM((30, rows, RANK), F),
        pltpu.VMEM((RHS, WIDTH), F),
    ]
    if fresh:
        out = [shape((RHS, WIDTH)), shape((DEVICES, RHS + 8, RANK)), made]
        scratch += [
            pltpu.VMEM(blocks.shape, jnp.int32),
            pltpu.VMEM(made.shape, F),
            pltpu.VMEM((16, RHS + 8, RANK), F),
        ]
    else:
        out = [shape((RHS, WIDTH)), shape((DEVICES, RANK)), shape((8, RANK))]
        scratch += [
            pltpu.VMEM(made.shape, F),
            pltpu.VMEM((DEVICES, 8, RANK), F),
            pltpu.VMEM((DEVICES, RANK), F),
        ]
    return call(
        functools.partial(down_kernel, fresh),
        "down_first" if fresh else "down_second",
        out,
        ids,
        [message, blocks, up_top, *sources],
        scratch,
        10**9,
    )


def finish_kernel(*refs):
    inputs, (solution_out, residual_out) = refs[:5], refs[5:7]
    held, (solution_held, residual_held, semaphores) = refs[7:12], refs[12:]
    copies = Copies(semaphores)
    wait_all([copies.start(source, target) for source, target in zip(inputs, held)])
    rows_ref, sums_ref, base_ref, image_ref, second_ref = held
    before = columns(sums_ref[...])
    rows = jnp.sum(rows_ref[...], 0, keepdims=True)
    after = columns(jnp.broadcast_to(rows, (8, RANK)))
    norm, curvature = before[0:RHS], before[RHS : 2 * RHS]
    step = norm / curvature
    norm_next, rm, bm, ri = [after[q * RHS : (q + 1) * RHS] for q in range(4)]
    turn = norm_next / norm
    second_curvature = rm + turn * (bm + ri + turn * curvature)
    second_step = norm_next / second_curvature
    base = base_ref[...]
    image = image_ref[...]
    residual = base - step * image
    direction = residual + turn * base
    moved = image - step * second_ref[...] + turn * image
    solution_held[...] = step * base + second_step * direction
    leave = [copies.start(solution_held, solution_out)]
    residual_held[...] = residual - second_step * moved
    leave.append(copies.start(residual_held, residual_out))
    wait_all(leave)


def finish(*inputs):
    out = [shape((RHS, WIDTH))] * 2
    return call(finish_kernel, "finish", out, None, inputs, scratch_for(inputs) + scratch_for(out), 10**6)


def beside(value):
    partner = [(i, i ^ 1) for i in range(DEVICES)]
    forward = [(i, i + 1) for i in range(1, DEVICES - 1, 2)]
    other = forward + [(target, source) for source, target in forward]
    return lax.ppermute(value, AXES, partner), lax.ppermute(value, AXES, other)


def everyone(copies):
    return lax.all_to_all(copies, AXES, 0, 0, tiled=True)


def local(
    points,
    right_side,
    interp,
    leaf_skel,
    up_one,
    skel_one,
    up_two,
    skel_two,
    up_three,
    skel_three,
    up_top,
    skel_top,
    near_list,
    far_three,
    far_top,
):
    device = lax.axis_index(AXES).astype(jnp.int32)
    fours = lax.dynamic_index_in_dim(far_top, device // 2, 0, False)
    fives = lax.dynamic_index_in_dim(far_top, NODES_FOUR + device // 4, 0, False) - NODES_FOUR
    ids = jnp.concatenate(
        [device[None], far_three[0], fours, fives, jnp.zeros((5,), jnp.int32), near_list.reshape(-1)]
    )
    weights = (interp, up_one, up_two, up_three)
    (message,) = first(points, right_side, weights, (leaf_skel, skel_one, skel_two, skel_three))
    message = everyone(message)
    part, right, left = near(True, ids, points, right_side, *beside(halo(points, right_side)))
    image, own_message, blocks = down(
        True, ids, message, skel_top, up_top, *weights, right_side, part
    )
    partner, other = beside(image)
    message = everyone(own_message)
    (part,) = near(False, ids, right, left, image, partner, other)
    second, rows, sums = down(
        False, ids, message, blocks, up_top, *weights, image, part, right_side
    )
    return tuple(finish(everyone(rows), sums, right_side, image, second))


def solution(mesh):
    both = ("leaf", "sub")
    placed = (
        P(None, both),
        P(None, both),
        P(both, None, None),
        P(both, None),
        P(both, None, None),
        P(both, None),
        P(both, None, None),
        P(both, None),
        P(both, None, None),
        P(both, None),
        P(),
        P(),
        P(both, None),
        P(both, None),
        P(),
    )
    return jax.shard_map(
        local,
        mesh=mesh,
        in_specs=placed,
        out_specs=(P(None, both), P(None, both)),
        check_vma=False,
    )
```

```python
import functools
import math

import jax
import jax.numpy as jnp
from jax import lax
from jax.experimental import pallas as pl
from jax.experimental.pallas import tpu as pltpu
from jax.sharding import PartitionSpec as P

LEAF = 512
DIMS = 32
RHS = 16
RANK = 128
LEAVES_HERE = 8
SLOTS = 12
WIDTH = LEAVES_HERE * LEAF
DEVICES = 128
NODES_FOUR = 64
TOP_SLOTS = 4
AT_THREE, AT_FOUR, AT_FIVE, AT_NEAR = 1, 3, 7, 16

RIDGE_TERM = 12.0
COORD_SCALE = math.sqrt(2.0 * math.log2(math.e) / 24.0)

AXES = ("leaf", "sub")
BF = jnp.bfloat16
F = jnp.float32
NN = (((1,), (0,)), ((), ()))
NT = (((1,), (1,)), ((), ()))
SMEM = pl.BlockSpec(memory_space=pltpu.SMEM)
ANY = pl.BlockSpec(memory_space=pl.ANY)


def shape(dims, dtype=F):
    return jax.ShapeDtypeStruct(dims, dtype)


def mm(a, b, dims=NN):
    return lax.dot_general(a, b, dims, preferred_element_type=F)


def split_two(x):
    high = x.astype(BF)
    return high, (x - high.astype(F)).astype(BF)


def split_three(x):
    high = x.astype(BF)
    rest = x - high.astype(F)
    mid = rest.astype(BF)
    return high, mid, (rest - mid.astype(F)).astype(BF)


def dot_split(a, w, dims=NN):
    ah, am = split_two(a)
    wh, wm = split_two(w)
    both = mm(jnp.concatenate([ah, am], 0), wh, dims)
    return both[:RHS] + both[RHS:] + mm(ah, wm, dims)


def operands(y):
    n = y.shape[1]
    h, m, l = split_three(y)
    half = 0.5 * jnp.sum(y * y, 0, keepdims=True)
    parts = [p.astype(F) for p in split_three(half)]
    one = [jnp.ones((1, n), F)] * 3
    pad = [jnp.zeros((10, n), F)]
    tail_left = jnp.concatenate(parts + one + pad, 0).astype(BF)
    tail_right = jnp.concatenate([-p for p in one + parts] + pad, 0).astype(BF)
    zero = jnp.zeros((48, n), BF)
    left = jnp.concatenate([h, h, m, h, l, m, tail_left, zero], 0)
    right = jnp.concatenate([h, m, h, l, h, m, tail_right, zero], 0)
    return left, right


def pick(parts, chosen):
    n = parts.shape[1]
    rows = lax.broadcasted_iota(jnp.int32, (n, RANK), 0)
    hot = jnp.where(rows == chosen, 1.0, 0.0).astype(BF)
    return mm(parts, hot).astype(BF)


def joined(parts):
    return parts[0:32].astype(F) + parts[32:64].astype(F) + parts[64:96].astype(F)


def parts_of(y):
    return jnp.concatenate(split_three(y), 0)


class Copies:
    def __init__(self, semaphores):
        self.semaphores = semaphores
        self.used = 0

    def start(self, source, target):
        copy = pltpu.make_async_copy(source, target, self.semaphores.at[self.used])
        self.used += 1
        copy.start()
        return copy


def wait_all(copies):
    for copy in copies:
        copy.wait()


def call(kernel, name, out, ids, inputs, scratch, flops, transcendentals=0):
    operands_given = ([ids] if ids is not None else []) + list(inputs)
    return pl.pallas_call(
        kernel,
        out_shape=out,
        in_specs=([SMEM] if ids is not None else []) + [ANY] * len(inputs),
        out_specs=[ANY] * len(out),
        scratch_shapes=scratch + [pltpu.SemaphoreType.DMA((48,))],
        compiler_params=pltpu.CompilerParams(vmem_limit_bytes=63 << 20),
        cost_estimate=pl.CostEstimate(
            flops=flops, bytes_accessed=6 << 20, transcendentals=transcendentals
        ),
        name=name,
    )(*operands_given)


def scratch_for(arrays):
    return [pltpu.VMEM(a.shape, a.dtype) for a in arrays]


def cols(a):
    return slice(a * LEAF, (a + 1) * LEAF)


def row_of_sums(products):
    folded = []
    for value in products:
        piece = value[:, 0:RANK]
        for t in range(1, WIDTH // RANK):
            piece = piece + value[:, t * RANK : (t + 1) * RANK]
        folded.append(piece)
    rest = RANK - RHS * len(folded)
    stacked = jnp.concatenate(folded + [jnp.zeros((rest, RANK), F)], 0)
    return jnp.sum(stacked.T, 0, keepdims=True)


def climb(field, interp, transfers):
    level = [dot_split(field[:, cols(a)], interp[a]) for a in range(LEAVES_HERE)]
    for ref in transfers:
        level = [
            dot_split(jnp.concatenate([level[2 * n], level[2 * n + 1]], 1), ref[n])
            for n in range(len(level) // 2)
        ]
    return level[0]


def first_kernel(*refs):
    inputs, (message_out, halo_out) = refs[:10], refs[10:12]
    held, (message, semaphores) = refs[12:22], refs[22:]
    copies = Copies(semaphores)
    arrive = [copies.start(source, target) for source, target in zip(inputs, held)]
    points, field, interp, one, two, three, leaf_pick, one_pick, two_pick, three_pick = held
    wait_all(arrive[0:2])
    leave = [
        copies.start(points, halo_out.at[0:DIMS, :]),
        copies.start(field, halo_out.at[DIMS : DIMS + RHS, :]),
    ]
    wait_all(arrive[6:])
    level = [
        pick(parts_of(points[:, cols(a)] * COORD_SCALE), leaf_pick[a : a + 1, :])
        for a in range(LEAVES_HERE)
    ]
    for ref in (one_pick, two_pick, three_pick):
        level = [
            pick(jnp.concatenate([level[2 * n], level[2 * n + 1]], 1), ref[n : n + 1, :])
            for n in range(len(level) // 2)
        ]
    message[:, RHS : RHS + DIMS, :] = jnp.broadcast_to(
        joined(level[0])[None], (message.shape[0], DIMS, RANK)
    )
    leave += send_copies(copies, message, message_out, slice(RHS, RHS + DIMS))
    wait_all(arrive[2:6])
    charges = climb(field, interp, (one, two, three))
    message[:, 0:RHS, :] = jnp.broadcast_to(charges[None], (message.shape[0], RHS, RANK))
    leave += send_copies(copies, message, message_out, slice(0, RHS))
    wait_all(leave)


def send_copies(copies, message, message_out, rows):
    count = message.shape[0]
    return [
        copies.start(message.at[:, rows], message_out.at[t * count : (t + 1) * count, rows])
        for t in range(DEVICES // count)
    ]


def first(points, right_side, weights, picks):
    inputs = [points, right_side, *weights, *picks]
    return call(
        first_kernel,
        "first_up",
        [shape((DEVICES, RHS + DIMS, RANK)), shape((DIMS + RHS, WIDTH))],
        None,
        inputs,
        scratch_for(inputs) + [pltpu.VMEM((16, RHS + DIMS, RANK), F)],
        10**9,
    )


def near_kernel(form, *refs):
    right, left, total, values, ea, eb, part, targets, origins, semaphores = refs[-10:]
    copies = Copies(semaphores)
    own_rights = right.at[0:LEAVES_HERE]
    beside_rights = right.at[LEAVES_HERE : 3 * LEAVES_HERE]
    if form == "own":
        ids_ref, points_in, field_in, part_out, right_out, left_out, points, field = refs[:8]
        arrive_field = copies.start(field_in, field)
        arrive_own = [copies.start(points_in, points)]
    elif form == "beside":
        ids_ref, left_in, part_in, partner_in, other_in, part_out, right_out = refs[:7]
        partner, other = refs[7:9]
    else:
        ids_ref, right_in, right_beside_in, left_in, field_in, partner_in, other_in, part_out = refs[:8]
        field, partner, other = refs[8:11]
        arrive_field = copies.start(field_in, field)
        arrive_own = [copies.start(left_in, left), copies.start(right_in, own_rights)]
    if form != "own":
        arrive_beside = [copies.start(partner_in, partner), copies.start(other_in, other)]
    if form == "beside":
        arrive_own = [copies.start(left_in, left), copies.start(part_in, part)]
    if form == "all":
        arrive_beside.append(copies.start(right_beside_in, beside_rights))
    first = ids_ref[0] * LEAVES_HERE
    empty = 3 * LEAVES_HERE
    beside_at = 128
    odd = ids_ref[0] % 2 == 1
    shift_low = jnp.where(odd, 2 * LEAVES_HERE, 3 * LEAVES_HERE)
    shift_high = jnp.where(odd, LEAVES_HERE, 0)

    def collect(a, counts):
        n, m = counts
        targets[n] = a
        origins[n] = a
        n = n + 1
        for slot in range(SLOTS):
            place = ids_ref[AT_NEAR + a * SLOTS + slot] - first
            inside = (place >= 0) & (place < LEAVES_HERE)
            targets[n] = a
            origins[n] = place
            n = n + (inside & (place != a)).astype(jnp.int32)
            targets[m] = a
            origins[m] = place + jnp.where(place < 0, shift_low, shift_high)
            m = m + jnp.logical_not(inside).astype(jnp.int32)
        return n, m

    own_end, beside_end = lax.fori_loop(
        0, LEAVES_HERE, collect, (jnp.int32(0), jnp.int32(beside_at))
    )
    for end in (own_end, beside_end):
        for extra in range(4):
            targets[end + extra] = 0
            origins[end + extra] = empty

    def take_values(source, at):
        for a in range(LEAVES_HERE):
            values[at + a] = jnp.concatenate(split_three(source[source.shape[0] - RHS :, cols(a)]), 0)

    def exponent(t):
        origin = origins[t]
        return mm(right[jnp.where(origin == empty, LEAVES_HERE if form == "beside" else 0, origin)], left[targets[t]])

    def add(t, e):
        a = targets[t]
        v = values[origins[t]]
        block = jnp.exp2(e)
        upper = block.astype(BF)
        lower = (block - upper.astype(F)).astype(BF)
        total[a, 0:32] += mm(v[:32], upper)
        total[a, 0:16] += mm(v[:16], lower)

    def run(start, end):
        ea[...] = exponent(start)

        def pair(t):
            eb[...] = exponent(t + 1)
            add(t, ea[...])
            ea[...] = exponent(t + 2)
            add(t + 1, eb[...])

        def eight(p, carry):
            for u in range(4):
                pair(start + 8 * p + 2 * u)
            return carry

        def two(p, carry):
            pair(middle + 2 * p)
            return carry

        eights = (end - start) // 8
        middle = start + 8 * eights
        lax.fori_loop(0, eights, eight, 0)
        lax.fori_loop(0, (end - middle + 1) // 2, two, 0)

    total[...] = jnp.zeros_like(total)
    values[empty] = jnp.zeros((3 * RHS, LEAF), BF)
    leave = []
    if form != "beside":
        wait_all([arrive_field])
        take_values(field, 0)
    if form != "own":
        wait_all(arrive_beside[:2])
        take_values(partner, LEAVES_HERE)
        take_values(other, 2 * LEAVES_HERE)
    if form == "beside":
        for side, source in enumerate((partner, other)):
            for a in range(LEAVES_HERE):
                y = source[0:DIMS, cols(a)] * COORD_SCALE
                right[(side + 1) * LEAVES_HERE + a] = operands(y)[1].T
        leave.append(copies.start(beside_rights, right_out))
    wait_all(arrive_own)
    if form == "own":
        for a in range(LEAVES_HERE):
            left_part, right_part = operands(points[:, cols(a)] * COORD_SCALE)
            left[a] = left_part
            right[a] = right_part.T
        leave.append(copies.start(left, left_out))
        leave.append(copies.start(own_rights, right_out))
    if form != "beside":
        run(0, own_end)
    if form == "all":
        wait_all(arrive_beside[2:])
    if form != "own":
        run(beside_at, beside_end)
    for a in range(LEAVES_HERE):
        result = total[a, 0:16] + total[a, 16:32]
        if form == "beside":
            result = part[:, cols(a)] + result
        part[:, cols(a)] = result
    leave.append(copies.start(part, part_out))
    wait_all(leave)


def near(form, ids, *inputs):
    right = shape((3 * LEAVES_HERE, LEAF, 256), BF)
    left = shape((LEAVES_HERE, 256, LEAF), BF)
    held = {"own": inputs, "beside": inputs[2:], "all": inputs[3:]}[form]
    made = {
        "own": [shape((LEAVES_HERE, LEAF, 256), BF), left],
        "beside": [shape((2 * LEAVES_HERE, LEAF, 256), BF)],
        "all": [],
    }[form]
    return call(
        functools.partial(near_kernel, form),
        "near_" + form,
        [shape((RHS, WIDTH))] + made,
        ids,
        inputs,
        scratch_for(held)
        + scratch_for([right, left])
        + [
            pltpu.VMEM((LEAVES_HERE, 32, LEAF), F),
            pltpu.VMEM((3 * LEAVES_HERE + 1, 3 * RHS, LEAF), BF),
            pltpu.VMEM((LEAF, LEAF), F),
            pltpu.VMEM((LEAF, LEAF), F),
            pltpu.VMEM((RHS, WIDTH), F),
            pltpu.SMEM((256,), jnp.int32),
            pltpu.SMEM((256,), jnp.int32),
        ],
        40 * 10**9,
        50 * LEAF * LEAF,
    )


def first_step(row_block):
    sums = columns(row_block)
    return sums[0:RHS] / sums[RHS : 2 * RHS]


def columns(row_block):
    return row_block.T[:, 0:1]


def down_kernel(fresh, *refs):
    ids_ref, message_in, blocks_in, up_top_in = refs[:4]
    if fresh:
        sources, (image_out, message_out, blocks_out) = refs[4:10], refs[10:13]
        refs = refs[13:]
    else:
        sources, (image_out, rows_out, sums_out) = refs[4:11], refs[11:14]
        refs = refs[14:]
    held, refs = refs[: len(sources)], refs[len(sources) :]
    weights, nodes, image, semaphores = refs[0], refs[1], refs[2], refs[-1]
    copies = Copies(semaphores)
    dev = ids_ref[0]
    node_four = dev // 2
    node_five = dev // 4
    threes = [ids_ref[AT_THREE + s] for s in range(2)]
    fours = [ids_ref[AT_FOUR + s] for s in range(TOP_SLOTS)]
    fives = [ids_ref[AT_FIVE + s] for s in range(TOP_SLOTS)]

    early = []
    if fresh:
        picks, made = refs[3], refs[4]
        early.append(copies.start(blocks_in, picks))
        blocks = made
    else:
        blocks, all_sums, row = refs[3], refs[4], refs[5]
        early.append(copies.start(blocks_in, blocks))
        arrive_sums = copies.start(message_in.at[:, RHS : RHS + 8, :], all_sums)
    for s, n in enumerate(fives):
        early.append(copies.start(message_in.at[pl.ds(4 * n, 4)], nodes.at[4 * s : 4 * s + 4]))
    for s, n in enumerate(fours):
        early.append(
            copies.start(message_in.at[pl.ds(2 * n, 2)], nodes.at[16 + 2 * s : 18 + 2 * s])
        )
    for s, n in enumerate(threes):
        early.append(copies.start(message_in.at[pl.ds(n, 1)], nodes.at[24 + s : 25 + s]))
    if fresh:
        early.append(copies.start(message_in.at[pl.ds(4 * node_five, 4)], nodes.at[26:30]))
    arrive = []
    for s, n in enumerate(fives):
        arrive.append(copies.start(up_top_in.at[pl.ds(2 * n, 2)], weights.at[3 * s : 3 * s + 2]))
        arrive.append(
            copies.start(
                up_top_in.at[pl.ds(NODES_FOUR + n, 1)], weights.at[3 * s + 2 : 3 * s + 3]
            )
        )
    for s, n in enumerate(fours + [node_four, NODES_FOUR + node_five]):
        arrive.append(copies.start(up_top_in.at[pl.ds(n, 1)], weights.at[12 + s : 13 + s]))
    arrive_held = [copies.start(source, target) for source, target in zip(sources, held)]
    interp, one, two, three, field, near_part = held[:6]
    wait_all(early)

    def pair_of(at, get):
        return jnp.concatenate([get(at), get(at + 1)], 1)

    if fresh:

        def base(at):
            return parts_of(nodes[at, RHS : RHS + DIMS, :])

        def four(at, n):
            return pick(pair_of(at, base), picks[pl.ds(n, 1), :])

        def five(at, n):
            both = jnp.concatenate([four(at, 2 * n), four(at + 2, 2 * n + 1)], 1)
            return pick(both, picks[pl.ds(NODES_FOUR + n, 1), :])

        def block(slot, own_left, other, differs):
            right = operands(joined(other))[1]
            made[slot] = jnp.exp2(mm(right.T, own_left)) * jnp.where(differs, 1.0, 0.0)

        own = operands(nodes[26 + dev % 4, RHS : RHS + DIMS, :])[0]
        for s, n in enumerate(threes):
            block(s, own, base(24 + s), n != dev)
        own = operands(joined(four(26 + 2 * (node_four % 2), node_four)))[0]
        for s, n in enumerate(fours):
            block(2 + s, own, four(16 + 2 * s, n), n != node_four)
        own = operands(joined(five(26, node_five)))[0]
        for s, n in enumerate(fives):
            block(6 + s, own, five(4 * s, n), n != node_five)
        leave = [copies.start(made, blocks_out)]
    else:
        leave = []

    def charge(at):
        return nodes[at, 0:RHS, :]

    field_three = jnp.zeros((RHS, RANK), F)
    for s in range(2):
        field_three = field_three + dot_split(charge(24 + s), blocks[s])
    wait_all(arrive)
    field_five = jnp.zeros((RHS, RANK), F)
    for s in range(TOP_SLOTS):
        lower = dot_split(pair_of(4 * s, charge), weights[3 * s])
        upper = dot_split(pair_of(4 * s + 2, charge), weights[3 * s + 1])
        q = dot_split(jnp.concatenate([lower, upper], 1), weights[3 * s + 2])
        field_five = field_five + dot_split(q, blocks[6 + s])
    field_four = jnp.zeros((RHS, RANK), F)
    for s in range(TOP_SLOTS):
        q = dot_split(pair_of(16 + 2 * s, charge), weights[12 + s])
        field_four = field_four + dot_split(q, blocks[2 + s])

    def half(at, side):
        return weights[at, pl.ds(pl.multiple_of(side * RANK, RANK), RANK), :]

    field_four = field_four + dot_split(field_five, half(17, node_four % 2), NT)
    level = [field_three + dot_split(field_four, half(16, dev % 2), NT)]
    wait_all(arrive_held)
    for ref in (three, two, one):
        spread = [dot_split(h, ref[n], NT) for n, h in enumerate(level)]
        level = [s[:, side * RANK : (side + 1) * RANK] for s in spread for side in range(2)]
    for a in range(LEAVES_HERE):
        far = dot_split(level[a], interp[a], NT)
        image[:, cols(a)] = RIDGE_TERM * field[:, cols(a)] + near_part[:, cols(a)] + far
    leave.append(copies.start(image, image_out))
    if fresh:
        message = refs[5]
        charges = climb(image, interp, (one, two, three))
        sums = row_of_sums([field[...] * field[...], field[...] * image[...]])
        block = jnp.concatenate([charges, sums, jnp.zeros((7, RANK), F)], 0)
        message[...] = jnp.broadcast_to(block[None], message.shape)
        leave += send_copies(copies, message, message_out, slice(0, RHS + 8))
    else:
        wait_all([arrive_sums])
        base_field = held[6]
        all_sums[0] = jnp.sum(all_sums[...], 0)
        step = first_step(all_sums[0])
        residual = base_field[...] - step * field[...]
        moved = field[...] - step * image[...]
        sums = row_of_sums(
            [residual * residual, residual * moved, base_field[...] * moved, residual * field[...]]
        )
        row[...] = jnp.broadcast_to(sums, row.shape)
        leave.append(copies.start(row, rows_out))
        leave.append(copies.start(all_sums.at[0], sums_out))
    wait_all(leave)


def down(fresh, ids, message, blocks, up_top, *sources):
    made = shape((2 + 2 * TOP_SLOTS, RANK, RANK))
    rows = message.shape[1]
    scratch = scratch_for(sources) + [
        pltpu.VMEM((18, 2 * RANK, RANK), F),
        pltpu.VMEM((30, rows, RANK), F),
        pltpu.VMEM((RHS, WIDTH), F),
    ]
    if fresh:
        out = [shape((RHS, WIDTH)), shape((DEVICES, RHS + 8, RANK)), made]
        scratch += [
            pltpu.VMEM(blocks.shape, jnp.int32),
            pltpu.VMEM(made.shape, F),
            pltpu.VMEM((16, RHS + 8, RANK), F),
        ]
    else:
        out = [shape((RHS, WIDTH)), shape((DEVICES, RANK)), shape((8, RANK))]
        scratch += [
            pltpu.VMEM(made.shape, F),
            pltpu.VMEM((DEVICES, 8, RANK), F),
            pltpu.VMEM((DEVICES, RANK), F),
        ]
    return call(
        functools.partial(down_kernel, fresh),
        "down_first" if fresh else "down_second",
        out,
        ids,
        [message, blocks, up_top, *sources],
        scratch,
        10**9,
    )


def finish_kernel(*refs):
    inputs, (solution_out, residual_out) = refs[:5], refs[5:7]
    held, (solution_held, residual_held, semaphores) = refs[7:12], refs[12:]
    copies = Copies(semaphores)
    wait_all([copies.start(source, target) for source, target in zip(inputs, held)])
    rows_ref, sums_ref, base_ref, image_ref, second_ref = held
    before = columns(sums_ref[...])
    rows = jnp.sum(rows_ref[...], 0, keepdims=True)
    after = columns(jnp.broadcast_to(rows, (8, RANK)))
    norm, curvature = before[0:RHS], before[RHS : 2 * RHS]
    step = norm / curvature
    norm_next, rm, bm, ri = [after[q * RHS : (q + 1) * RHS] for q in range(4)]
    turn = norm_next / norm
    second_curvature = rm + turn * (bm + ri + turn * curvature)
    second_step = norm_next / second_curvature
    base = base_ref[...]
    image = image_ref[...]
    residual = base - step * image
    direction = residual + turn * base
    moved = image - step * second_ref[...] + turn * image
    solution_held[...] = step * base + second_step * direction
    leave = [copies.start(solution_held, solution_out)]
    residual_held[...] = residual - second_step * moved
    leave.append(copies.start(residual_held, residual_out))
    wait_all(leave)


def finish(*inputs):
    out = [shape((RHS, WIDTH))] * 2
    return call(finish_kernel, "finish", out, None, inputs, scratch_for(inputs) + scratch_for(out), 10**6)


def beside(value):
    partner = [(i, i ^ 1) for i in range(DEVICES)]
    forward = [(i, i + 1) for i in range(1, DEVICES - 1, 2)]
    other = forward + [(target, source) for source, target in forward]
    return lax.ppermute(value, AXES, partner), lax.ppermute(value, AXES, other)


def everyone(copies):
    return lax.all_to_all(copies, AXES, 0, 0, tiled=True)


def local(
    points,
    right_side,
    interp,
    leaf_skel,
    up_one,
    skel_one,
    up_two,
    skel_two,
    up_three,
    skel_three,
    up_top,
    skel_top,
    near_list,
    far_three,
    far_top,
):
    device = lax.axis_index(AXES).astype(jnp.int32)
    fours = lax.dynamic_index_in_dim(far_top, device // 2, 0, False)
    fives = lax.dynamic_index_in_dim(far_top, NODES_FOUR + device // 4, 0, False) - NODES_FOUR
    ids = jnp.concatenate(
        [device[None], far_three[0], fours, fives, jnp.zeros((5,), jnp.int32), near_list.reshape(-1)]
    )
    weights = (interp, up_one, up_two, up_three)
    message, halo = first(
        points, right_side, weights, (leaf_skel, skel_one, skel_two, skel_three)
    )
    partner, other = beside(halo)
    message = everyone(message)
    part, right, left = near("own", ids, points, right_side)
    part, right_beside = near("beside", ids, left, part, partner, other)
    image, own_message, blocks = down(
        True, ids, message, skel_top, up_top, *weights, right_side, part
    )
    partner, other = beside(image)
    message = everyone(own_message)
    (part,) = near("all", ids, right, right_beside, left, image, partner, other)
    second, rows, sums = down(
        False, ids, message, blocks, up_top, *weights, image, part, right_side
    )
    return tuple(finish(everyone(rows), sums, right_side, image, second))


def solution(mesh):
    both = ("leaf", "sub")
    placed = (
        P(None, both),
        P(None, both),
        P(both, None, None),
        P(both, None),
        P(both, None, None),
        P(both, None),
        P(both, None, None),
        P(both, None),
        P(both, None, None),
        P(both, None),
        P(),
        P(),
        P(both, None),
        P(both, None),
        P(),
    )
    return jax.shard_map(
        local,
        mesh=mesh,
        in_specs=placed,
        out_specs=(P(None, both), P(None, both)),
        check_vma=False,
    )
```
